128 devices in a mesh: ao: 16 (over z, x), aux: 8 (over y, core).
Axes of the slice: x: 4, y: 4, z: 4, core: 2. Of those that a mesh axis runs over, the one named last changes fastest.
Arguments:
- integrals: bfloat16 [16, 8, 8, 128, 16, 128], P('ao', 'aux'), may hold values from -0.25 to 0.25
- block_list: int32 [16, 16, 2], P('ao'), may hold values from 0 to 7, as said below
- pair_count: int32 [16, 16], P('ao'), may hold values from 0 to 2, as said below
- occupied: bfloat16 [16, 8, 16, 2, 128, 128], P('ao'), may hold values from -0.125 to 0.125
- virtual: bfloat16 [8, 128, 128], P('aux'), may hold values from -0.5 to 0.5
Outputs:
- response: float32 [16, 16], P('ao', 'aux')
The draws below stay inside these ranges and needn't reach their ends.
Inputs may be any that keep to these rules, and one draw needn't show every extreme that they name: For every i and d the 2 entries block_list[i,d,:] are different. pair_count[i,i] = 2 for every i.
All inputs are finite; a program needn't handle non-finite values.
Results may differ from the reference program's by a relative error of at most 0.0042.
Values may be sent and summed in bfloat16 or wider, within the bound.
No kernel may reach another device: no remote copies, remote signals or barrier semaphores. Data moves between devices by JAX's collectives and lax.ppermute only.
A program may use at most 128 MiB of HBM per device.

```python
import jax
import jax.numpy as jnp
from jax import lax

BS = 128
NB_DEV = 8
SLOT = 2
AB = 16
N_AO = 16
N_AUX = 8


def draw_block_list(key, part):
    key = jax.random.fold_in(key, 5)
    scores = jax.random.randint(key, (N_AO, N_AO, NB_DEV), 0, 1 << 20)
    scores = scores * NB_DEV + jnp.arange(NB_DEV, dtype=jnp.int32)[None, None, :]
    ordering = jnp.argsort(scores, axis=-1, stable=True)
    return ordering[:, :, :SLOT].astype(jnp.int32)


def draw_pair_count(key, part):
    key = jax.random.fold_in(key, 11)
    counts = jax.random.randint(key, (N_AO, N_AO), 0, SLOT + 1)
    diagonal = jnp.eye(N_AO, dtype=jnp.int32)
    counts = jnp.where(diagonal > 0, SLOT, counts)
    return counts.astype(jnp.int32)


def block_scale(key, shape, pieces, least, high):
    loudness, own = 1.0, jax.random.fold_in(key, 6)
    for position, blocks in pieces:
        steps = jnp.exp(jax.random.uniform(jax.random.fold_in(own, position), (blocks,), jnp.float32, least / len(pieces), high / len(pieces)))
        loudness = loudness * jnp.repeat(steps, shape[position] // blocks).reshape([-1 if axis == position else 1 for axis in range(len(shape))])
    return loudness


def normal_values(key, extent, width, bound, split=(), kind=jnp.bfloat16):
    gain = block_scale(key, extent, split, -0.22, 0.18) if split else 1.0
    drawn = jax.random.normal(key, extent, jnp.float32) * width * gain
    return jnp.minimum(jnp.maximum(drawn, -bound), bound).astype(kind)


def setup_inputs(seed: int = 0) -> dict:
    seeds = jax.random.split(jax.random.key(seed), 6)
    return {
        "integrals": normal_values(seeds[0], (N_AO, N_AUX, NB_DEV, BS, AB, BS), ((BS * (NB_DEV * N_AO * N_AUX) ** 0.5) ** -0.5), 0.25, ((0, 16), (1, 8))),
        "block_list": draw_block_list(jax.random.fold_in(seeds[5], 71), 0),
        "pair_count": draw_pair_count(jax.random.fold_in(seeds[5], 71), 0),
        "occupied": normal_values(seeds[3], (N_AO, NB_DEV, N_AO, SLOT, BS, BS), (N_AO * SLOT * BS // 2) ** -0.5, 0.125, ((0, 16),)),
        "virtual": normal_values(seeds[4], (N_AUX, BS, BS), BS ** -0.5, 0.5, ((0, 8),)),
    }


def reference(integrals, block_list, pair_count, occupied, virtual):
    slot_ids = jnp.arange(SLOT, dtype=jnp.int32)
    usable = slot_ids[None, None, :] < pair_count[:, :, None]
    owners = jnp.arange(N_AO, dtype=jnp.int32)

    def one_pair(response, step_index):
        target = step_index // N_AUX
        nu_block = step_index % N_AUX
        chosen_blocks = block_list[:, target, :]
        sent_tiles = integrals[owners[:, None], nu_block, chosen_blocks].astype(jnp.float32)
        usable_here = usable[:, target, :]
        sent_tiles = jnp.where(usable_here[:, :, None, None, None], sent_tiles, 0.0)
        couplings = occupied[target].astype(jnp.float32)
        occupied_part = jnp.einsum('aiklm,ikmpn->alpn', couplings, sent_tiles).astype(jnp.bfloat16)
        virtual_block = virtual[nu_block].astype(jnp.float32)
        mixed = jnp.einsum('alpn,ns->alps', occupied_part.astype(jnp.float32), virtual_block).astype(jnp.bfloat16)
        own_tiles = integrals[target, nu_block].astype(jnp.float32)
        response = response + jnp.einsum('alps,alqs->pq', mixed.astype(jnp.float32), own_tiles)
        return response, None

    steps_all = jnp.arange(N_AO * N_AUX, dtype=jnp.int32)
    response, unused = lax.scan(one_pair, jnp.zeros((AB, AB), jnp.float32), steps_all)
    return response
```

```python
import functools

import jax
import jax.numpy as jnp
from jax import lax
from jax.experimental import pallas as pl
from jax.experimental.pallas import tpu as pltpu
from jax.sharding import PartitionSpec as P

BS = 128
NB = 8
AB = 16
WIDE = AB * BS
ROWS = NB * BS
AXES = ("ao", "aux")
SIDE = 4
N_AO = 16
CHUNKS = 2
PER = NB // CHUNKS
G = 2
ALWAYS = 6
STEPS = 8
RELAY = 32
SEND, TAKE, NEAR = 16, 64, 128
VMEM_BYTES = 56 * 1024 * 1024


def shift(ring, step):
    pairs = []
    for z in range(SIDE):
        for x in range(SIDE):
            for aux in range(8):
                along_x = (aux % 2 == 0) != ring
                to = z * SIDE + (x + step) % SIDE if along_x else (z + step) % SIDE * SIDE + x
                pairs.append(((z * SIDE + x) * 8 + aux, to * 8 + aux))
    return pairs


def across(array, step):
    return lax.ppermute(array, AXES, shift(False, step))


def around(array, step):
    return lax.ppermute(array, AXES, shift(True, step))


def index_of(core, t, e):
    return jnp.where(core == 0, t * SIDE + e, e * SIDE + t)


def ring_plan(lists, core, e):
    def count(ts, td):
        td = index_of(core, td % SIDE, e)
        total = 0
        for other in range(SIDE):
            total = total + lists[index_of(core, ts, other), 32 + td]
        return total

    up1 = [count(t, t + 1) for t in range(SIDE)]
    down1 = [count(t, t + 3) for t in range(SIDE)]
    far = [count(t, t + 2) for t in range(SIDE)]

    def loads(ups):
        downs = [far[t] - ups[t] for t in range(SIDE)]
        up = [jnp.maximum(up1[t] + ups[t], 2 * G) + ups[(t + 3) % SIDE] for t in range(SIDE)]
        down = [jnp.maximum(down1[t] + downs[t], 2 * G) + downs[(t + 1) % SIDE] for t in range(SIDE)]
        return up, down

    def longest(ups):
        up, down = loads(ups)
        return functools.reduce(jnp.maximum, up + down)

    plain = [far[t] // 2 for t in range(SIDE)]
    ups = list(plain)
    for _ in range(2):
        for t in range(SIDE):
            up, down = loads(ups)
            excess = jnp.maximum(up[t], up[(t + 1) % SIDE]) - jnp.maximum(down[t], down[(t + 3) % SIDE])
            move = jnp.where(excess >= 0, excess // 2, -((-excess) // 2))
            ups[t] = jnp.clip(ups[t] - move, 0, far[t])
    better = longest(ups) < longest(plain)
    ups = [jnp.where(better, a, b) for a, b in zip(ups, plain)]
    return up1, down1, far, ups, longest(ups)


def pick(values, t):
    out = values[0]
    for s in range(1, SIDE):
        out = jnp.where(t == s, values[s], out)
    return out


def plan_kernel(lists, where, table):
    ao, aux = where[0], where[1]
    core = aux % 2
    z, x = ao // SIDE, ao % SIDE
    t = jnp.where(core == 0, z, x)
    e = jnp.where(core == 0, x, z)

    def ring(r, most):
        return jnp.maximum(most, ring_plan(lists, r // SIDE, r % SIDE)[4])

    table[0] = lax.fori_loop(0, 2 * SIDE, ring, jnp.int32(0))
    up1, down1, far, ups, _ = ring_plan(lists, core, e)
    downs = [far[s] - ups[s] for s in range(SIDE)]

    for r in range(G * STEPS):
        for way in range(2):
            table[SEND + 16 * way + r] = 0
            table[TAKE + 16 * way + r] = -1

    def each(ts, td, then):
        ts, td = ts % SIDE, td % SIDE
        d = index_of(core, td, e)
        n = jnp.int32(0)
        for other in range(SIDE):
            i = index_of(core, ts, other)
            count = lists[i, 32 + d]
            for k in range(2):
                @pl.when(k < count)
                def _(n=n, other=other, i=i, k=k):
                    then(n, other, i, k, lists[i, 2 * d + k])
                n = n + jnp.where(k < count, 1, 0)
        return n

    def held(other, block):
        return (other - e + SIDE) % SIDE * NB + block

    my_up, my_down = pick(ups, t), pick(downs, t)

    def send_far(n, other, i, k, block):
        @pl.when(n < my_up)
        def _():
            table[SEND + n] = held(other, block)

        @pl.when(n >= my_up)
        def _():
            table[SEND + 16 + n - my_up] = held(other, block)

    def send_up(n, other, i, k, block):
        table[SEND + my_up + n] = held(other, block)

    def send_down(n, other, i, k, block):
        table[SEND + 16 + my_down + n] = held(other, block)

    each(t, t + 2, send_far)
    each(t, t + 1, send_up)
    each(t, t + 3, send_down)
    before, after = (t + 3) % SIDE, (t + 1) % SIDE
    for way, first, number in (
        (0, jnp.maximum(my_up + pick(up1, t), 2 * G), pick(ups, before)),
        (1, jnp.maximum(my_down + pick(down1, t), 2 * G), pick(downs, after)),
    ):
        def relay(j, _, way=way, first=first):
            table[SEND + 16 * way + first + j] = RELAY + j
            return 0
        lax.fori_loop(0, number, relay, 0)

    def take_up(n, other, i, k, block):
        table[TAKE + pick(ups, before) + n] = 2 * i + k

    def take_down(n, other, i, k, block):
        table[TAKE + 16 + pick(downs, after) + n] = 2 * i + k

    opposite = (t + 2) % SIDE
    first_up = jnp.maximum(pick(ups, before) + pick(up1, before), 2 * G)
    first_down = jnp.maximum(pick(downs, after) + pick(down1, after), 2 * G)
    far_up = pick(ups, opposite)

    def take_far(n, other, i, k, block):
        @pl.when(n < far_up)
        def _():
            table[TAKE + first_up + n] = 2 * i + k

        @pl.when(n >= far_up)
        def _():
            table[TAKE + 16 + first_down + n - far_up] = 2 * i + k

    each(t + 3, t, take_up)
    each(t + 1, t, take_down)
    each(t + 2, t, take_far)

    def near(n, other, i, k, block):
        table[NEAR + n] = held(other, block) * 32 + 2 * i + k

    table[1] = each(t, t, near)


def plan(lists, where):
    smem = pl.BlockSpec(memory_space=pltpu.SMEM)
    return pl.pallas_call(
        plan_kernel,
        out_shape=jax.ShapeDtypeStruct((256,), jnp.int32),
        in_specs=[smem, smem],
        out_specs=smem,
    )(lists, where)


def pack_kernel(step, relays, table, *refs):
    tiles = refs[:4 * CHUNKS]
    came = refs[4 * CHUNKS:4 * CHUNKS + 2 * relays]
    outs = refs[4 * CHUNKS + 2 * relays:4 * CHUNKS + 2 * relays + 2]
    sems = refs[-1]
    waits = []
    for way in range(2):
        for h in range(G):
            code = table[SEND + 16 * way + G * step + h]
            dst = outs[way].at[h]
            sem = sems.at[G * way + h]
            for c, tile in enumerate(tiles):
                @pl.when(code // PER == c)
                def _(tile=tile, dst=dst, sem=sem, code=code):
                    pltpu.make_async_copy(tile.at[code % PER], dst, sem).start()
            for q in range(relays):
                for g in range(G):
                    @pl.when(code == RELAY + G * q + g)
                    def _(q=q, g=g, way=way, dst=dst, sem=sem):
                        pltpu.make_async_copy(came[2 * q + way].at[g], dst, sem).start()
            waits.append(pltpu.make_async_copy(tiles[0].at[0], dst, sem))
    for copy in waits:
        copy.wait()


def pack(step, table, tiles, came):
    relays = max(step - 1, 0)
    smem = pl.BlockSpec(memory_space=pltpu.SMEM)
    hbm = pl.BlockSpec(memory_space=pl.ANY)
    operands = [chunk for tile in tiles for chunk in tile]
    for q in range(relays):
        operands += came[q]
    shape = jax.ShapeDtypeStruct((G, BS, WIDE), jnp.bfloat16)
    return pl.pallas_call(
        functools.partial(pack_kernel, step, relays),
        out_shape=[shape, shape],
        in_specs=[smem] + [hbm] * len(operands),
        out_specs=[hbm, hbm],
        scratch_shapes=[pltpu.SemaphoreType.DMA((2 * G,))],
        cost_estimate=pl.CostEstimate(flops=0, bytes_accessed=4 * 1024 * 1024, transcendentals=0),
    )(table, *operands)


def gather(own_c, left, right, sems, wanted):
    n = jnp.int32(0)
    for ok, slot, start in wanted:
        @pl.when(ok)
        def _(n=n, slot=slot, start=start):
            at = pl.ds(pl.multiple_of(n * BS, BS), BS)
            pltpu.make_async_copy(own_c.at[:, slot // 2, slot % 2], left.at[:, :, at], sems.at[0]).start()
            start(right.at[at], sems.at[1])
        n = n + jnp.where(ok, 1, 0)
    return n


def contract(own_c, left, right, sems, n, acc, clear):
    def arrive(_, carry):
        at = pl.ds(0, BS)
        pltpu.make_async_copy(own_c.at[:, 0, 0], left.at[:, :, at], sems.at[0]).wait()
        pltpu.make_async_copy(right.at[at], right.at[at], sems.at[1]).wait()
        return carry

    lax.fori_loop(0, n, arrive, 0)

    @pl.when(n % 2 == 1)
    def _():
        at = pl.ds(pl.multiple_of(n * BS, BS), BS)
        left[:, :, at] = jnp.zeros((NB, BS, BS), jnp.bfloat16)
        right[at, :] = jnp.zeros((BS, WIDE), jnp.bfloat16)

    if clear:
        acc[...] = jnp.zeros_like(acc)

    def pair(p, carry):
        at = pl.ds(pl.multiple_of(p * 2 * BS, 2 * BS), 2 * BS)
        for j in range(WIDE // 512):
            cols = slice(j * 512, (j + 1) * 512)
            acc[:, cols] += jnp.dot(
                left[:, :, at].reshape(ROWS, 2 * BS), right[at, cols], preferred_element_type=jnp.float32
            )
        return carry

    lax.fori_loop(0, (n + 1) // 2, pair, 0)


def near_kernel(table, own_c, *refs):
    tiles = refs[:4 * CHUNKS]
    out, left, right, acc, sems = refs[4 * CHUNKS:]
    wanted = []
    for s in range(2 * SIDE):
        entry = table[NEAR + s]
        code = entry // 32

        def start(dst, sem, code=code):
            for c, tile in enumerate(tiles):
                @pl.when(code // PER == c)
                def _():
                    pltpu.make_async_copy(tile.at[code % PER], dst, sem).start()

        wanted.append((s < table[1], entry % 32, start))
    n = gather(own_c, left, right, sems, wanted)
    contract(own_c, left, right, sems, n, acc, True)
    copy = pltpu.make_async_copy(acc, out, sems.at[2])
    copy.start()
    copy.wait()


def from_steps(table, steps, came):
    wanted = []
    for q, step in enumerate(steps):
        for way in range(2):
            for h in range(G):
                slot = table[TAKE + 16 * way + G * step + h]

                def start(dst, sem, q=q, way=way, h=h):
                    pltpu.make_async_copy(came[2 * q + way].at[h], dst, sem).start()

                wanted.append((slot >= 0, jnp.maximum(slot, 0), start))
    return wanted


def middle_kernel(steps, table, own_c, before, *refs):
    came = refs[:2 * len(steps)]
    out, left, right, acc, sems = refs[2 * len(steps):]
    fetch = pltpu.make_async_copy(before, acc, sems.at[2])
    fetch.start()
    n = gather(own_c, left, right, sems, from_steps(table, steps, came))
    fetch.wait()
    contract(own_c, left, right, sems, n, acc, False)
    copy = pltpu.make_async_copy(acc, out, sems.at[2])
    copy.start()
    copy.wait()


def last_kernel(steps, table, own_c, before, turn, first, second, *refs):
    came = refs[:2 * len(steps)]
    out, left, right, acc, rows, mixed, total, sems = refs[2 * len(steps):]
    fetch = pltpu.make_async_copy(before, acc, sems.at[2])
    fetch.start()
    n = gather(own_c, left, right, sems, from_steps(table, steps, came))
    own = []
    for c, chunk in enumerate((first, second)):
        copy = pltpu.make_async_copy(chunk, rows.at[pl.ds(c * PER, PER)], sems.at[3 + c])
        copy.start()
        own.append(copy)
    fetch.wait()
    contract(own_c, left, right, sems, n, acc, False)

    @pl.loop(0, WIDE // 256)
    def _(j):
        cols = pl.ds(pl.multiple_of(j * 256, 256), 256)
        part = acc[:, cols].astype(jnp.bfloat16)
        mixed[:, cols] = jnp.dot(part, turn[...], preferred_element_type=jnp.float32).astype(jnp.bfloat16)

    for copy in own:
        copy.wait()
    total[...] = jnp.zeros_like(total)

    @pl.loop(0, ROWS // 32)
    def _(j):
        def stacked(load):
            halves = []
            for h in range(2):
                at = pl.multiple_of(j * 32 + h * 16, 16)
                halves.append(jnp.concatenate([load(at, slice(p * BS, (p + 1) * BS)) for p in range(AB)], axis=0))
            return jnp.concatenate(halves, axis=1)

        block = j // (BS // 32)
        total[...] += lax.dot_general(
            stacked(lambda at, cols: mixed[pl.ds(at, 16), cols]),
            stacked(lambda at, cols: rows[block, pl.ds(pl.multiple_of(at - block * BS, 16), 16), cols]),
            (((1,), (1,)), ((), ())),
            preferred_element_type=jnp.float32,
        )

    r = lax.broadcasted_iota(jnp.int32, (256, 256), 0)
    c = lax.broadcasted_iota(jnp.int32, (256, 256), 1)
    kept = jnp.where(r % 16 == c % 16, total[...], 0.0)
    kept = kept.reshape(16, 16, 256).sum(axis=1)
    rr = lax.broadcasted_iota(jnp.int32, (256, 16), 0)
    cc = lax.broadcasted_iota(jnp.int32, (256, 16), 1)
    pick_q = jnp.where(rr // 16 == cc, 1.0, 0.0)
    out[...] = jnp.dot(kept, pick_q, preferred_element_type=jnp.float32, precision=lax.Precision.HIGHEST)


def run(kernel, table, own_c, operands, vmem_operands, blocks, last):
    smem = pl.BlockSpec(memory_space=pltpu.SMEM)
    vmem = pl.BlockSpec(memory_space=pltpu.VMEM)
    hbm = pl.BlockSpec(memory_space=pl.ANY)
    scratch = [
        pltpu.VMEM((NB, BS, blocks * BS), jnp.bfloat16),
        pltpu.VMEM((blocks * BS, WIDE), jnp.bfloat16),
        pltpu.VMEM((ROWS, WIDE), jnp.float32),
    ]
    if last:
        scratch += [
            pltpu.VMEM((NB, BS, WIDE), jnp.bfloat16),
            pltpu.VMEM((ROWS, WIDE), jnp.bfloat16),
            pltpu.VMEM((256, 256), jnp.float32),
        ]
    scratch.append(pltpu.SemaphoreType.DMA((5,)))
    shape = (16, 16) if last else (ROWS, WIDE)
    return pl.pallas_call(
        kernel,
        out_shape=jax.ShapeDtypeStruct(shape, jnp.float32),
        in_specs=[smem, hbm] + [vmem if k in vmem_operands else hbm for k in range(len(operands))],
        out_specs=vmem if last else hbm,
        scratch_shapes=scratch,
        compiler_params=pltpu.CompilerParams(vmem_limit_bytes=VMEM_BYTES),
        cost_estimate=pl.CostEstimate(
            flops=blocks * ROWS * BS * WIDE, bytes_accessed=16 * 1024 * 1024 + blocks * 768 * 1024, transcendentals=0
        ),
    )(table, own_c, *operands)


def per_device(integrals, block_list, pair_count, occupied, virtual):
    own_c = occupied[0]
    ao = lax.axis_index("ao")
    aux = lax.axis_index("aux")
    where = jnp.stack([ao, aux]).astype(jnp.int32)

    lists = jnp.concatenate([block_list.reshape(1, 32), pair_count], axis=1)
    lists = lax.all_gather(lists, "ao", axis=0, tiled=True)

    own = [integrals[0, 0, c * PER:(c + 1) * PER].reshape(PER, BS, WIDE) for c in range(CHUNKS)]
    last = [across(own[c], 1) for c in range(CHUNKS)]
    following = [across(own[c], -1) for c in range(CHUNKS)]
    far = [across(last[0], 1), across(following[1], -1)]
    tiles = [own, following, far, last]

    table = plan(lists, where)
    longest = table[0]

    came = []

    def step(q, came):
        up, down = pack(q, table, tiles, came)
        return [around(up, 1), around(down, -1)]

    for q in range(ALWAYS):
        came.append(step(q, came))

    flat = [chunk for tile in tiles for chunk in tile]
    acc = run(near_kernel, table, own_c, flat, (), 2 * SIDE, False)
    for some in ((0, 1, 2), (3, 4)):
        acc = run(
            functools.partial(middle_kernel, some), table, own_c,
            [acc] + [b for q in some for b in came[q]], (), 2 * G * len(some), False,
        )

    block = virtual[0]
    zero = jnp.zeros_like(block)
    turn = jnp.concatenate(
        [jnp.concatenate([block, zero], axis=1), jnp.concatenate([zero, block], axis=1)], axis=0
    )

    def finish(some, came, acc, turn):
        return run(
            functools.partial(last_kernel, some), table, own_c,
            [acc, turn] + own + [b for q in some for b in came[q]], (1,), 2 * G * len(some), True,
        )

    def short(came, acc, turn):
        return finish((ALWAYS - 1,), came, acc, turn)

    def full(came, acc, turn):
        came = list(came)
        for q in range(ALWAYS, STEPS):
            came.append(step(q, came))
        return finish(tuple(range(ALWAYS - 1, STEPS)), came, acc, turn)

    partial = lax.cond(longest > G * ALWAYS, full, short, came, acc, turn)

    pieces = lax.all_to_all(partial.reshape(128, 2), AXES, split_axis=0, concat_axis=0, tiled=True)
    return pieces.sum(axis=0).reshape(1, 2)


def solution(mesh):
    placed = (
        P("ao", "aux", None, None, None, None),
        P("ao", None, None),
        P("ao", None),
        P("ao", None, None, None, None, None),
        P("aux", None, None),
    )
    return jax.shard_map(
        per_device, mesh=mesh, in_specs=placed, out_specs=P("ao", "aux"), check_vma=False
    )
```

```python
import functools

import jax
import jax.numpy as jnp
from jax import lax
from jax.experimental import pallas as pl
from jax.experimental.pallas import tpu as pltpu
from jax.sharding import PartitionSpec as P

BS = 128
NB = 8
AB = 16
WIDE = AB * BS
ROWS = NB * BS
AXES = ("ao", "aux")
SIDE = 4
N_AO = 16
LIST = 48
CHUNKS = 2
PER = NB // CHUNKS
G = 2
ALWAYS = 6
STEPS = 8
DELAY = 3
RELAY = 32
SEND, TAKE, NEAR = 16, 64, 128
VMEM_BYTES = 56 * 1024 * 1024


def shift(ring, step):
    pairs = []
    for z in range(SIDE):
        for x in range(SIDE):
            for aux in range(8):
                along_x = (aux % 2 == 0) != ring
                to = z * SIDE + (x + step) % SIDE if along_x else (z + step) % SIDE * SIDE + x
                pairs.append(((z * SIDE + x) * 8 + aux, to * 8 + aux))
    return pairs


def across(array, step):
    return lax.ppermute(array, AXES, shift(False, step))


def around(array, step):
    return lax.ppermute(array, AXES, shift(True, step))


def index_of(core, t, e):
    return jnp.where(core == 0, t * SIDE + e, e * SIDE + t)


def ring_plan(lists, core, e):
    def count(ts, td):
        td = index_of(core, td % SIDE, e)
        total = 0
        for other in range(SIDE):
            total = total + lists[index_of(core, ts, other), 32 + td]
        return total

    up1 = [count(t, t + 1) for t in range(SIDE)]
    down1 = [count(t, t + 3) for t in range(SIDE)]
    far = [count(t, t + 2) for t in range(SIDE)]

    def loads(ups):
        downs = [far[t] - ups[t] for t in range(SIDE)]
        up = [jnp.maximum(up1[t] + ups[t], DELAY * G) + ups[(t + 3) % SIDE] for t in range(SIDE)]
        down = [jnp.maximum(down1[t] + downs[t], DELAY * G) + downs[(t + 1) % SIDE] for t in range(SIDE)]
        return up, down

    def longest(ups):
        up, down = loads(ups)
        return functools.reduce(jnp.maximum, up + down)

    plain = [far[t] // 2 for t in range(SIDE)]
    ups = list(plain)
    for _ in range(2):
        for t in range(SIDE):
            up, down = loads(ups)
            excess = jnp.maximum(up[t], up[(t + 1) % SIDE]) - jnp.maximum(down[t], down[(t + 3) % SIDE])
            move = jnp.where(excess >= 0, excess // 2, -((-excess) // 2))
            ups[t] = jnp.clip(ups[t] - move, 0, far[t])
    better = longest(ups) < longest(plain)
    ups = [jnp.where(better, a, b) for a, b in zip(ups, plain)]
    return up1, down1, far, ups, longest(ups)


def pick(values, t):
    out = values[0]
    for s in range(1, SIDE):
        out = jnp.where(t == s, values[s], out)
    return out


def plan_kernel(came, where, table, lists):
    ao, aux = where[0], where[1]
    core = aux % 2
    z, x = ao // SIDE, ao % SIDE
    t = jnp.where(core == 0, z, x)
    e = jnp.where(core == 0, x, z)

    def place(r, _):
        i = index_of(core, (t - r // SIDE + SIDE) % SIDE, (e - r % SIDE + SIDE) % SIDE)
        for c in range(LIST):
            lists[i, c] = came[r, c]
        return 0

    lax.fori_loop(0, N_AO, place, 0)

    def ring(r, most):
        return jnp.maximum(most, ring_plan(lists, r // SIDE, r % SIDE)[4])

    table[0] = lax.fori_loop(0, 2 * SIDE, ring, jnp.int32(0))
    up1, down1, far, ups, _ = ring_plan(lists, core, e)
    downs = [far[s] - ups[s] for s in range(SIDE)]

    for r in range(G * STEPS):
        for way in range(2):
            table[SEND + 16 * way + r] = 0
            table[TAKE + 16 * way + r] = -1

    def each(ts, td, then):
        ts, td = ts % SIDE, td % SIDE
        d = index_of(core, td, e)
        n = jnp.int32(0)
        for other in range(SIDE):
            i = index_of(core, ts, other)
            count = lists[i, 32 + d]
            for k in range(2):
                @pl.when(k < count)
                def _(n=n, other=other, i=i, k=k):
                    then(n, other, i, k, lists[i, 2 * d + k])
                n = n + jnp.where(k < count, 1, 0)
        return n

    def held(other, block):
        return (other - e + SIDE) % SIDE * NB + block

    my_up, my_down = pick(ups, t), pick(downs, t)

    def send_far(n, other, i, k, block):
        @pl.when(n < my_up)
        def _():
            table[SEND + n] = held(other, block)

        @pl.when(n >= my_up)
        def _():
            table[SEND + 16 + n - my_up] = held(other, block)

    def send_up(n, other, i, k, block):
        table[SEND + my_up + n] = held(other, block)

    def send_down(n, other, i, k, block):
        table[SEND + 16 + my_down + n] = held(other, block)

    each(t, t + 2, send_far)
    each(t, t + 1, send_up)
    each(t, t + 3, send_down)
    before, after = (t + 3) % SIDE, (t + 1) % SIDE
    for way, first, number in (
        (0, jnp.maximum(my_up + pick(up1, t), DELAY * G), pick(ups, before)),
        (1, jnp.maximum(my_down + pick(down1, t), DELAY * G), pick(downs, after)),
    ):
        def relay(j, _, way=way, first=first):
            table[SEND + 16 * way + first + j] = RELAY + j
            return 0
        lax.fori_loop(0, number, relay, 0)

    def take_up(n, other, i, k, block):
        table[TAKE + pick(ups, before) + n] = 2 * i + k

    def take_down(n, other, i, k, block):
        table[TAKE + 16 + pick(downs, after) + n] = 2 * i + k

    opposite = (t + 2) % SIDE
    first_up = jnp.maximum(pick(ups, before) + pick(up1, before), DELAY * G)
    first_down = jnp.maximum(pick(downs, after) + pick(down1, after), DELAY * G)
    far_up = pick(ups, opposite)

    def take_far(n, other, i, k, block):
        @pl.when(n < far_up)
        def _():
            table[TAKE + first_up + n] = 2 * i + k

        @pl.when(n >= far_up)
        def _():
            table[TAKE + 16 + first_down + n - far_up] = 2 * i + k

    each(t + 3, t, take_up)
    each(t + 1, t, take_down)
    each(t + 2, t, take_far)

    def near(n, other, i, k, block):
        table[NEAR + n] = held(other, block) * 32 + 2 * i + k

    table[1] = each(t, t, near)


def plan(lists, where):
    smem = pl.BlockSpec(memory_space=pltpu.SMEM)
    return pl.pallas_call(
        plan_kernel,
        out_shape=jax.ShapeDtypeStruct((256,), jnp.int32),
        in_specs=[smem, smem],
        out_specs=smem,
        scratch_shapes=[pltpu.SMEM((N_AO, LIST), jnp.int32)],
    )(lists, where)


def pack_kernel(step, relays, table, *refs):
    tiles = refs[:4 * CHUNKS]
    came = refs[4 * CHUNKS:4 * CHUNKS + 2 * relays]
    outs = refs[4 * CHUNKS + 2 * relays:4 * CHUNKS + 2 * relays + 2]
    sems = refs[-1]
    waits = []
    for way in range(2):
        for h in range(G):
            code = table[SEND + 16 * way + G * step + h]
            dst = outs[way].at[h]
            sem = sems.at[G * way + h]
            for c, tile in enumerate(tiles):
                @pl.when(code // PER == c)
                def _(tile=tile, dst=dst, sem=sem, code=code):
                    pltpu.make_async_copy(tile.at[code % PER], dst, sem).start()
            for q in range(relays):
                for g in range(G):
                    @pl.when(code == RELAY + G * q + g)
                    def _(q=q, g=g, way=way, dst=dst, sem=sem):
                        pltpu.make_async_copy(came[2 * q + way].at[g], dst, sem).start()
            waits.append(pltpu.make_async_copy(tiles[0].at[0], dst, sem))
    for copy in waits:
        copy.wait()


def pack(step, table, tiles, came):
    relays = max(step - DELAY + 1, 0)
    smem = pl.BlockSpec(memory_space=pltpu.SMEM)
    vmem = pl.BlockSpec(memory_space=pltpu.VMEM)
    hbm = pl.BlockSpec(memory_space=pl.ANY)
    operands = [chunk for tile in tiles for chunk in tile]
    for q in range(relays):
        operands += came[q]
    shape = jax.ShapeDtypeStruct((G, BS, WIDE), jnp.bfloat16)
    return pl.pallas_call(
        functools.partial(pack_kernel, step, relays),
        out_shape=[shape, shape],
        in_specs=[smem] + [hbm] * len(operands),
        out_specs=[vmem, vmem],
        scratch_shapes=[pltpu.SemaphoreType.DMA((2 * G,))],
        cost_estimate=pl.CostEstimate(flops=0, bytes_accessed=1024, transcendentals=0),
    )(table, *operands)


def gather(own_c, left, right, sems, wanted):
    n = jnp.int32(0)
    for ok, slot, start in wanted:
        @pl.when(ok)
        def _(n=n, slot=slot, start=start):
            at = pl.ds(pl.multiple_of(n * BS, BS), BS)
            pltpu.make_async_copy(own_c.at[:, slot // 2, slot % 2], left.at[:, :, at], sems.at[0]).start()
            start(right.at[at], sems.at[1])
        n = n + jnp.where(ok, 1, 0)
    return n


def contract(own_c, left, right, sems, n, acc, clear):
    def arrive(_, carry):
        at = pl.ds(0, BS)
        pltpu.make_async_copy(own_c.at[:, 0, 0], left.at[:, :, at], sems.at[0]).wait()
        pltpu.make_async_copy(right.at[at], right.at[at], sems.at[1]).wait()
        return carry

    lax.fori_loop(0, n, arrive, 0)

    @pl.when(n % 2 == 1)
    def _():
        at = pl.ds(pl.multiple_of(n * BS, BS), BS)
        left[:, :, at] = jnp.zeros((NB, BS, BS), jnp.bfloat16)
        right[at, :] = jnp.zeros((BS, WIDE), jnp.bfloat16)

    if clear:
        acc[...] = jnp.zeros_like(acc)

    def pair(p, carry):
        at = pl.ds(pl.multiple_of(p * 2 * BS, 2 * BS), 2 * BS)
        for j in range(WIDE // 512):
            cols = slice(j * 512, (j + 1) * 512)
            acc[:, cols] += jnp.dot(
                left[:, :, at].reshape(ROWS, 2 * BS), right[at, cols], preferred_element_type=jnp.float32
            )
        return carry

    lax.fori_loop(0, (n + 1) // 2, pair, 0)


def from_steps(table, steps, came):
    wanted = []
    for q, step in enumerate(steps):
        for way in range(2):
            for h in range(G):
                slot = table[TAKE + 16 * way + G * step + h]

                def start(dst, sem, q=q, way=way, h=h):
                    pltpu.make_async_copy(came[2 * q + way].at[h], dst, sem).start()

                wanted.append((slot >= 0, jnp.maximum(slot, 0), start))
    return wanted


def sum_kernel(near, steps, clear, table, own_c, *refs):
    refs = list(refs)
    before = None if clear else refs.pop(0)
    tiles = {m: [refs.pop(0) for _ in range(CHUNKS)] for m in near}
    came = [refs.pop(0) for _ in range(2 * len(steps))]
    out, left, right, acc, sems = refs
    fetch = None
    if not clear:
        fetch = pltpu.make_async_copy(before, acc, sems.at[2])
        fetch.start()
    wanted = from_steps(table, steps, came)
    for s in range(2 * SIDE if near else 0):
        entry = table[NEAR + s]
        code = entry // 32
        here = jnp.bool_(False)
        for m in near:
            here = jnp.logical_or(here, code // NB == m)

        def start(dst, sem, code=code):
            for m in near:
                for c, chunk in enumerate(tiles[m]):
                    @pl.when(code // PER == m * CHUNKS + c)
                    def _():
                        pltpu.make_async_copy(chunk.at[code % PER], dst, sem).start()

        wanted.append((jnp.logical_and(s < table[1], here), entry % 32, start))
    n = gather(own_c, left, right, sems, wanted)
    if not clear:
        fetch.wait()
    contract(own_c, left, right, sems, n, acc, clear)
    copy = pltpu.make_async_copy(acc, out, sems.at[2])
    copy.start()
    copy.wait()


def last_kernel(steps, table, own_c, before, turn, first, second, *refs):
    came = refs[:2 * len(steps)]
    out, left, right, acc, rows, mixed, total, sems = refs[2 * len(steps):]
    fetch = pltpu.make_async_copy(before, acc, sems.at[2])
    fetch.start()
    n = gather(own_c, left, right, sems, from_steps(table, steps, came))
    own = []
    for c, chunk in enumerate((first, second)):
        copy = pltpu.make_async_copy(chunk, rows.at[pl.ds(c * PER, PER)], sems.at[3 + c])
        copy.start()
        own.append(copy)
    fetch.wait()
    contract(own_c, left, right, sems, n, acc, False)

    @pl.loop(0, WIDE // 256)
    def _(j):
        cols = pl.ds(pl.multiple_of(j * 256, 256), 256)
        part = acc[:, cols].astype(jnp.bfloat16)
        mixed[:, cols] = jnp.dot(part, turn[...], preferred_element_type=jnp.float32).astype(jnp.bfloat16)

    for copy in own:
        copy.wait()
    total[...] = jnp.zeros_like(total)

    @pl.loop(0, ROWS // 32, unroll=4)
    def _(j):
        def stacked(load):
            halves = []
            for h in range(2):
                at = pl.multiple_of(j * 32 + h * 16, 16)
                halves.append(jnp.concatenate([load(at, slice(p * BS, (p + 1) * BS)) for p in range(AB)], axis=0))
            return jnp.concatenate(halves, axis=1)

        block = j // (BS // 32)
        total[...] += lax.dot_general(
            stacked(lambda at, cols: mixed[pl.ds(at, 16), cols]),
            stacked(lambda at, cols: rows[block, pl.ds(pl.multiple_of(at - block * BS, 16), 16), cols]),
            (((1,), (1,)), ((), ())),
            preferred_element_type=jnp.float32,
        )

    r = lax.broadcasted_iota(jnp.int32, (256, 256), 0)
    c = lax.broadcasted_iota(jnp.int32, (256, 256), 1)
    kept = jnp.where(r % 16 == c % 16, total[...], 0.0)
    kept = kept.reshape(16, 16, 256).sum(axis=1)
    rr = lax.broadcasted_iota(jnp.int32, (256, 16), 0)
    cc = lax.broadcasted_iota(jnp.int32, (256, 16), 1)
    pick_q = jnp.where(rr // 16 == cc, 1.0, 0.0)
    out[...] = jnp.dot(kept, pick_q, preferred_element_type=jnp.float32, precision=lax.Precision.HIGHEST)


def run(kernel, table, own_c, operands, vmem_operands, blocks, last):
    smem = pl.BlockSpec(memory_space=pltpu.SMEM)
    vmem = pl.BlockSpec(memory_space=pltpu.VMEM)
    hbm = pl.BlockSpec(memory_space=pl.ANY)
    scratch = [
        pltpu.VMEM((NB, BS, blocks * BS), jnp.bfloat16),
        pltpu.VMEM((blocks * BS, WIDE), jnp.bfloat16),
        pltpu.VMEM((ROWS, WIDE), jnp.float32),
    ]
    if last:
        scratch += [
            pltpu.VMEM((NB, BS, WIDE), jnp.bfloat16),
            pltpu.VMEM((ROWS, WIDE), jnp.bfloat16),
            pltpu.VMEM((256, 256), jnp.float32),
        ]
    scratch.append(pltpu.SemaphoreType.DMA((5,)))
    shape = (16, 16) if last else (ROWS, WIDE)
    return pl.pallas_call(
        kernel,
        out_shape=jax.ShapeDtypeStruct(shape, jnp.float32),
        in_specs=[smem, hbm] + [vmem if k in vmem_operands else hbm for k in range(len(operands))],
        out_specs=vmem if last else hbm,
        scratch_shapes=scratch,
        compiler_params=pltpu.CompilerParams(vmem_limit_bytes=VMEM_BYTES),
        cost_estimate=pl.CostEstimate(
            flops=blocks * ROWS * BS * WIDE, bytes_accessed=16 * 1024 * 1024 + blocks * 768 * 1024, transcendentals=0
        ),
    )(table, own_c, *operands)


def flatten_kernel(tile, out):
    out[0] = tile[0, 0, 0].reshape(BS, WIDE)


def flatten(integrals, chunk):
    return pl.pallas_call(
        flatten_kernel,
        grid=(PER,),
        out_shape=jax.ShapeDtypeStruct((PER, BS, WIDE), jnp.bfloat16),
        in_specs=[pl.BlockSpec((1, 1, 1, BS, AB, BS), lambda b: (0, 0, chunk * PER + b, 0, 0, 0))],
        out_specs=pl.BlockSpec((1, BS, WIDE), lambda b: (b, 0, 0)),
    )(integrals)


def per_device(integrals, block_list, pair_count, occupied, virtual):
    own_c = occupied[0]
    ao = lax.axis_index("ao")
    aux = lax.axis_index("aux")
    where = jnp.stack([ao, aux]).astype(jnp.int32)

    own = [flatten(integrals, c) for c in range(CHUNKS)]
    lists = jnp.concatenate([block_list.reshape(1, 32), pair_count], axis=1)
    own[0], lists = lax.optimization_barrier((own[0], lists))
    lists = jnp.concatenate([lists, around(lists, 1)], axis=0)
    lists = jnp.concatenate([lists, around(lists, 2)], axis=0)
    lists = lax.ppermute(lists, "aux", [(g, g ^ 1) for g in range(8)])
    lists = jnp.concatenate([lists, around(lists, 1)], axis=0)
    lists = jnp.concatenate([lists, around(lists, 2)], axis=0)
    table = plan(lists, where)
    longest = table[0]

    last = [across(own[c], 1) for c in range(CHUNKS)]
    following = [across(own[c], -1) for c in range(CHUNKS)]
    first, table = lax.optimization_barrier((last[0], table))
    far = [across(first, 1), across(following[1], -1)]
    tiles = [own, following, far, last]

    came = []

    def add(acc, near, some):
        blocks = [chunk for tile in near for chunk in tiles[tile]] + [b for q in some for b in came[q]]
        return run(
            functools.partial(sum_kernel, near, some, acc is None), table, own_c,
            ([] if acc is None else [acc]) + blocks, (), 2 * SIDE + 2 * G * len(some), False,
        )

    acc = add(None, (0, 1, 3), ())
    table, acc, *far = lax.optimization_barrier((table, acc, *far))
    tiles[2] = far
    ready = pack(0, table, tiles, came)
    for q in range(ALWAYS):
        if q + 1 < ALWAYS:
            following = pack(q + 1, table, tiles, came)
            if q > 0:
                ready, following = lax.optimization_barrier((ready, following))
        came.append([around(ready[0], 1), around(ready[1], -1)])
        ready = following
        if q == 3:
            acc = add(acc, (2,), (0, 1))
            table, acc = lax.optimization_barrier((table, acc))
        if q == 5:
            acc = add(acc, (), (2, 3))

    block = virtual[0]
    zero = jnp.zeros_like(block)
    turn = jnp.concatenate(
        [jnp.concatenate([block, zero], axis=1), jnp.concatenate([zero, block], axis=1)], axis=0
    )

    def finish(some, came, acc, turn):
        return run(
            functools.partial(last_kernel, some), table, own_c,
            [acc, turn] + own + [b for q in some for b in came[q]], (1,), 2 * G * len(some), True,
        )

    def short(came, acc, turn):
        return finish((ALWAYS - 2, ALWAYS - 1), came, acc, turn)

    def full(came, acc, turn):
        came = list(came)
        for q in range(ALWAYS, STEPS):
            up, down = pack(q, table, tiles, came)
            came.append([around(up, 1), around(down, -1)])
        return finish(tuple(range(ALWAYS - 2, STEPS)), came, acc, turn)

    partial = lax.cond(longest > G * ALWAYS, full, short, came, acc, turn)

    pieces = lax.all_to_all(partial.reshape(128, 2), AXES, split_axis=0, concat_axis=0, tiled=True)
    return pieces.sum(axis=0).reshape(1, 2)


def solution(mesh):
    placed = (
        P("ao", "aux", None, None, None, None),
        P("ao", None, None),
        P("ao", None),
        P("ao", None, None, None, None, None),
        P("aux", None, None),
    )
    return jax.shard_map(
        per_device, mesh=mesh, in_specs=placed, out_specs=P("ao", "aux"), check_vma=False
    )
```

```python
import functools

import jax
import jax.numpy as jnp
from jax import lax
from jax.experimental import pallas as pl
from jax.experimental.pallas import tpu as pltpu
from jax.sharding import PartitionSpec as P

BS = 128
NB = 8
AB = 16
WIDE = AB * BS
ROWS = NB * BS
AXES = ("ao", "aux")
SIDE = 4
N_AO = 16
LIST = 48
CHUNKS = 2
PER = NB // CHUNKS
G = 3
ALWAYS = 4
STEPS = 6
DELAY = 2
RELAY = 32
FIRST = G
FAR = 2
ORDER = (0, 1, 3, FAR)
PARTS = 4
SEND, TAKE, NEAR = 16, 64, 128
VMEM_BYTES = 56 * 1024 * 1024


def shift(ring, step):
    pairs = []
    for z in range(SIDE):
        for x in range(SIDE):
            for aux in range(8):
                along_x = (aux % 2 == 0) != ring
                to = z * SIDE + (x + step) % SIDE if along_x else (z + step) % SIDE * SIDE + x
                pairs.append(((z * SIDE + x) * 8 + aux, to * 8 + aux))
    return pairs


def across(array, step):
    return lax.ppermute(array, AXES, shift(False, step))


def around(array, step):
    return lax.ppermute(array, AXES, shift(True, step))


def index_of(core, t, e):
    return jnp.where(core == 0, t * SIDE + e, e * SIDE + t)


def pick(values, t):
    out = values[0]
    for s in range(1, SIDE):
        out = jnp.where(t == s, values[s], out)
    return out


def ring_plan(lists, core, e):
    def count(ts, td):
        td = index_of(core, td % SIDE, e)
        near = lists[index_of(core, ts, (e + ORDER[0]) % SIDE), 32 + td]
        for rel in ORDER[1:-1]:
            near = near + lists[index_of(core, ts, (e + rel) % SIDE), 32 + td]
        return near, near + lists[index_of(core, ts, (e + FAR) % SIDE), 32 + td]

    ones = [[count(t, t + step) for t in range(SIDE)] for step in (1, 3)]
    twos = [count(t, t + 2) for t in range(SIDE)]

    def layout(ups):
        ways = []
        for way, sender in ((0, 3), (1, 1)):
            two, two_near, gap, early, late, own, held_up = [], [], [], [], [], [], []
            for t in range(SIDE):
                if way == 0:
                    h = ups[t]
                    hn = jnp.minimum(h, twos[t][0])
                else:
                    h = twos[t][1] - ups[t]
                    hn = jnp.maximum(twos[t][0] - ups[t], 0)
                u = jnp.maximum(FIRST - hn, 0)
                us = jnp.minimum(u, ones[way][t][0])
                two.append(h)
                two_near.append(hn)
                gap.append(u)
                early.append(us)
                late.append(u + h)
                own.append(u + h + ones[way][t][1] - us)
                held_up.append(DELAY * G + jnp.where(h > hn, u, 0))
            relay = [jnp.maximum(own[t], held_up[(t + sender) % SIDE]) for t in range(SIDE)]
            length = [relay[t] + two[(t + sender) % SIDE] for t in range(SIDE)]
            ways.append(dict(two=two, two_near=two_near, gap=gap, early=early, late=late, relay=relay, length=length))
        return ways

    def longest(ups):
        up, down = layout(ups)
        return functools.reduce(jnp.maximum, up["length"] + down["length"])

    plain = [twos[t][1] // 2 for t in range(SIDE)]
    ups = list(plain)
    for _ in range(2):
        for t in range(SIDE):
            up, down = (way["length"] for way in layout(ups))
            excess = jnp.maximum(up[t], up[(t + 1) % SIDE]) - jnp.maximum(down[t], down[(t + 3) % SIDE])
            move = jnp.where(excess >= 0, excess // 2, -((-excess) // 2))
            ups[t] = jnp.clip(ups[t] - move, 0, twos[t][1])
    better = longest(ups) < longest(plain)
    ups = [jnp.where(better, a, b) for a, b in zip(ups, plain)]
    return ups, layout(ups), longest(ups)


def plan_kernel(came, where, table, lists):
    ao, aux = where[0], where[1]
    core = aux % 2
    z, x = ao // SIDE, ao % SIDE
    t = jnp.where(core == 0, z, x)
    e = jnp.where(core == 0, x, z)

    def place(r, _):
        i = index_of(core, (t - r // SIDE + SIDE) % SIDE, (e - r % SIDE + SIDE) % SIDE)
        for c in range(LIST):
            lists[i, c] = came[r, c]
        return 0

    lax.fori_loop(0, N_AO, place, 0)

    def ring(r, most):
        return jnp.maximum(most, ring_plan(lists, r // SIDE, r % SIDE)[2])

    table[0] = lax.fori_loop(0, 2 * SIDE, ring, jnp.int32(0))
    ups, ways, _ = ring_plan(lists, core, e)

    for r in range(G * STEPS):
        for way in range(2):
            table[SEND + 24 * way + r] = 0
            table[TAKE + 24 * way + r] = -1

    def each(ts, td, then):
        ts, td = ts % SIDE, td % SIDE
        d = index_of(core, td, e)
        n = jnp.int32(0)
        for rel in ORDER:
            i = index_of(core, ts, (e + rel) % SIDE)
            count = lists[i, 32 + d]
            for k in range(2):
                @pl.when(k < count)
                def _(n=n, i=i, k=k, rel=rel):
                    then(n, rel * NB + lists[i, 2 * d + k], 2 * i + k)
                n = n + jnp.where(k < count, 1, 0)
        return n

    def at_two(way, s, n):
        return n + jnp.where(n >= pick(way["two_near"], s), pick(way["gap"], s), 0)

    def at_one(way, s, n):
        early = pick(way["early"], s)
        return n + jnp.where(n < early, pick(way["two_near"], s), pick(way["late"], s) - early)

    my_up = pick(ups, t)

    def send_two(n, held, slot):
        @pl.when(n < my_up)
        def _():
            table[SEND + at_two(ways[0], t, n)] = held

        @pl.when(n >= my_up)
        def _():
            table[SEND + 24 + at_two(ways[1], t, n - my_up)] = held

    each(t, t + 2, send_two)
    opposite = (t + 2) % SIDE
    far_up = pick(ups, opposite)
    for way, step in ((0, 1), (1, 3)):
        sender = (t + 4 - step) % SIDE

        def send_one(n, held, slot, way=way):
            table[SEND + 24 * way + at_one(ways[way], t, n)] = held

        each(t, t + step, send_one)

        def relay(j, _, way=way, sender=sender):
            table[SEND + 24 * way + pick(ways[way]["relay"], t) + j] = RELAY + at_two(ways[way], sender, j)
            return 0

        lax.fori_loop(0, pick(ways[way]["two"], sender), relay, 0)

        def take_one(n, held, slot, way=way, sender=sender):
            table[TAKE + 24 * way + at_one(ways[way], sender, n)] = slot

        each(sender, t, take_one)

    def take_two(n, held, slot):
        @pl.when(n < far_up)
        def _():
            table[TAKE + pick(ways[0]["relay"], (t + 3) % SIDE) + n] = slot

        @pl.when(n >= far_up)
        def _():
            table[TAKE + 24 + pick(ways[1]["relay"], (t + 1) % SIDE) + n - far_up] = slot

    each(opposite, t, take_two)

    def near(n, held, slot):
        table[NEAR + n] = held * 32 + slot

    table[1] = each(t, t, near)


def plan(lists, where):
    smem = pl.BlockSpec(memory_space=pltpu.SMEM)
    return pl.pallas_call(
        plan_kernel,
        out_shape=jax.ShapeDtypeStruct((256,), jnp.int32),
        in_specs=[smem, smem],
        out_specs=smem,
        scratch_shapes=[pltpu.SMEM((N_AO, LIST), jnp.int32)],
    )(lists, where)


def pack_kernel(step, held, relays, table, *refs):
    refs = list(refs)
    tiles = {m: [refs.pop(0) for _ in range(CHUNKS)] for m in held}
    came = [refs.pop(0) for _ in range(2 * relays)]
    up, down, sems = refs
    waits = []
    for way, out in enumerate((up, down)):
        for h in range(G):
            code = table[SEND + 24 * way + G * step + h]
            dst = out.at[h]
            sem = sems.at[G * way + h]
            for m in held:
                for c, tile in enumerate(tiles[m]):
                    @pl.when(code // PER == m * CHUNKS + c)
                    def _(tile=tile, dst=dst, sem=sem, code=code):
                        pltpu.make_async_copy(tile.at[code % PER], dst, sem).start()
            for q in range(relays):
                for g in range(G):
                    @pl.when(code == RELAY + G * q + g)
                    def _(q=q, g=g, way=way, dst=dst, sem=sem):
                        pltpu.make_async_copy(came[2 * q + way].at[g], dst, sem).start()
            waits.append(pltpu.make_async_copy(tiles[0][0].at[0], dst, sem))
    for copy in waits:
        copy.wait()


def pack(step, table, tiles, came):
    relays = max(step - DELAY + 1, 0)
    held = [m for m in ORDER if G * step >= FIRST or m != FAR]
    smem = pl.BlockSpec(memory_space=pltpu.SMEM)
    vmem = pl.BlockSpec(memory_space=pltpu.VMEM)
    hbm = pl.BlockSpec(memory_space=pl.ANY)
    operands = [chunk for m in held for chunk in tiles[m]]
    for q in range(relays):
        operands += came[q]
    shape = jax.ShapeDtypeStruct((G, BS, WIDE), jnp.bfloat16)
    return pl.pallas_call(
        functools.partial(pack_kernel, step, held, relays),
        out_shape=[shape, shape],
        in_specs=[smem] + [hbm] * len(operands),
        out_specs=[vmem, vmem],
        scratch_shapes=[pltpu.SemaphoreType.DMA((2 * G,))],
        cost_estimate=pl.CostEstimate(flops=0, bytes_accessed=1024, transcendentals=0),
    )(table, *operands)


def gather(own_c, left, right, sems, wanted):
    n = jnp.int32(0)
    for ok, slot, start in wanted:
        @pl.when(ok)
        def _(n=n, slot=slot, start=start):
            at = pl.ds(pl.multiple_of(n * BS, BS), BS)
            pltpu.make_async_copy(own_c.at[:, slot // 2, slot % 2], left.at[:, :, at], sems.at[0]).start()
            start(right.at[at], sems.at[1])
        n = n + jnp.where(ok, 1, 0)
    return n


def arrive(own_c, left, right, sems, n):
    def one(_, carry):
        at = pl.ds(0, BS)
        pltpu.make_async_copy(own_c.at[:, 0, 0], left.at[:, :, at], sems.at[0]).wait()
        pltpu.make_async_copy(right.at[at], right.at[at], sems.at[1]).wait()
        return carry

    lax.fori_loop(0, n, one, 0)

    @pl.when(n % 2 == 1)
    def _():
        at = pl.ds(pl.multiple_of(n * BS, BS), BS)
        left[:, :, at] = jnp.zeros((NB, BS, BS), jnp.bfloat16)
        right[at, :] = jnp.zeros((BS, WIDE), jnp.bfloat16)


def contract(left, right, n, acc, cols):
    def pair(p, carry):
        at = pl.ds(pl.multiple_of(p * 2 * BS, 2 * BS), 2 * BS)
        acc[:, cols] += jnp.dot(
            left[:, :, at].reshape(ROWS, 2 * BS), right[at, cols], preferred_element_type=jnp.float32
        )
        return carry

    lax.fori_loop(0, (n + 1) // 2, pair, 0)


def from_steps(table, steps, came):
    wanted = []
    for q, step in enumerate(steps):
        for way in range(2):
            for h in range(G):
                slot = table[TAKE + 24 * way + G * step + h]

                def start(dst, sem, q=q, way=way, h=h):
                    pltpu.make_async_copy(came[2 * q + way].at[h], dst, sem).start()

                wanted.append((slot >= 0, jnp.maximum(slot, 0), start))
    return wanted


def sum_kernel(near, steps, clear, table, own_c, *refs):
    refs = list(refs)
    before = None if clear else refs.pop(0)
    tiles = {m: [refs.pop(0) for _ in range(CHUNKS)] for m in near}
    came = [refs.pop(0) for _ in range(2 * len(steps))]
    out, left, right, acc, sems = refs
    wanted = from_steps(table, steps, came)
    for s in range(2 * SIDE if near else 0):
        entry = table[NEAR + s]
        code = entry // 32
        here = jnp.bool_(False)
        for m in near:
            here = jnp.logical_or(here, code // NB == m)

        def start(dst, sem, code=code):
            for m in near:
                for c, chunk in enumerate(tiles[m]):
                    @pl.when(code // PER == m * CHUNKS + c)
                    def _():
                        pltpu.make_async_copy(chunk.at[code % PER], dst, sem).start()

        wanted.append((jnp.logical_and(s < table[1], here), entry % 32, start))
    n = gather(own_c, left, right, sems, wanted)
    parts = [slice(j * WIDE // PARTS, (j + 1) * WIDE // PARTS) for j in range(PARTS)]
    fetches = []
    for j, cols in enumerate(parts):
        if clear:
            acc[:, cols] = jnp.zeros((ROWS, WIDE // PARTS), jnp.float32)
        else:
            copy = pltpu.make_async_copy(before.at[:, cols], acc.at[:, cols], sems.at[2 + j])
            copy.start()
            fetches.append(copy)
    arrive(own_c, left, right, sems, n)
    stores = []
    for j, cols in enumerate(parts):
        if not clear:
            fetches[j].wait()
        contract(left, right, n, acc, cols)
        copy = pltpu.make_async_copy(acc.at[:, cols], out.at[:, cols], sems.at[2 + j])
        copy.start()
        stores.append(copy)
    for copy in stores:
        copy.wait()


def last_kernel(steps, table, own_c, before, turn, first, second, *refs):
    came = refs[:2 * len(steps)]
    out, left, right, acc, rows, mixed, total, sems = refs[2 * len(steps):]
    n = gather(own_c, left, right, sems, from_steps(table, steps, came))
    fetches = []
    for j in range(PARTS):
        cols = pl.ds(j * WIDE // PARTS, WIDE // PARTS)
        copy = pltpu.make_async_copy(before.at[:, cols], acc.at[:, cols], sems.at[2 + j])
        copy.start()
        fetches.append(copy)
    own = []
    for c, chunk in enumerate((first, second)):
        copy = pltpu.make_async_copy(chunk, rows.at[pl.ds(c * PER, PER)], sems.at[2 + PARTS + c])
        copy.start()
        own.append(copy)
    arrive(own_c, left, right, sems, n)
    for j, fetch in enumerate(fetches):
        fetch.wait()
        cols = slice(j * WIDE // PARTS, (j + 1) * WIDE // PARTS)
        contract(left, right, n, acc, cols)
        for k in range(WIDE // PARTS // 256):
            here = slice(cols.start + k * 256, cols.start + (k + 1) * 256)
            part = acc[:, here].astype(jnp.bfloat16)
            mixed[:, here] = jnp.dot(part, turn[...], preferred_element_type=jnp.float32).astype(jnp.bfloat16)

    for copy in own:
        copy.wait()
    total[...] = jnp.zeros_like(total)

    @pl.loop(0, ROWS // 32, unroll=4)
    def _(j):
        def stacked(load):
            halves = []
            for h in range(2):
                at = pl.multiple_of(j * 32 + h * 16, 16)
                halves.append(jnp.concatenate([load(at, slice(p * BS, (p + 1) * BS)) for p in range(AB)], axis=0))
            return jnp.concatenate(halves, axis=1)

        block = j // (BS // 32)
        total[...] += lax.dot_general(
            stacked(lambda at, cols: mixed[pl.ds(at, 16), cols]),
            stacked(lambda at, cols: rows[block, pl.ds(pl.multiple_of(at - block * BS, 16), 16), cols]),
            (((1,), (1,)), ((), ())),
            preferred_element_type=jnp.float32,
        )

    r = lax.broadcasted_iota(jnp.int32, (256, 256), 0)
    c = lax.broadcasted_iota(jnp.int32, (256, 256), 1)
    kept = jnp.where(r % 16 == c % 16, total[...], 0.0)
    kept = kept.reshape(16, 16, 256).sum(axis=1)
    rr = lax.broadcasted_iota(jnp.int32, (256, 16), 0)
    cc = lax.broadcasted_iota(jnp.int32, (256, 16), 1)
    pick_q = jnp.where(rr // 16 == cc, 1.0, 0.0)
    out[...] = jnp.dot(kept, pick_q, preferred_element_type=jnp.float32, precision=lax.Precision.HIGHEST)


def run(kernel, table, own_c, operands, vmem_operands, blocks, last):
    smem = pl.BlockSpec(memory_space=pltpu.SMEM)
    vmem = pl.BlockSpec(memory_space=pltpu.VMEM)
    hbm = pl.BlockSpec(memory_space=pl.ANY)
    scratch = [
        pltpu.VMEM((NB, BS, blocks * BS), jnp.bfloat16),
        pltpu.VMEM((blocks * BS, WIDE), jnp.bfloat16),
        pltpu.VMEM((ROWS, WIDE), jnp.float32),
    ]
    if last:
        scratch += [
            pltpu.VMEM((NB, BS, WIDE), jnp.bfloat16),
            pltpu.VMEM((ROWS, WIDE), jnp.bfloat16),
            pltpu.VMEM((256, 256), jnp.float32),
        ]
    scratch.append(pltpu.SemaphoreType.DMA((4 + PARTS,)))
    shape = (16, 16) if last else (ROWS, WIDE)
    return pl.pallas_call(
        kernel,
        out_shape=jax.ShapeDtypeStruct(shape, jnp.float32),
        in_specs=[smem, hbm] + [vmem if k in vmem_operands else hbm for k in range(len(operands))],
        out_specs=vmem if last else hbm,
        scratch_shapes=scratch,
        compiler_params=pltpu.CompilerParams(vmem_limit_bytes=VMEM_BYTES),
        cost_estimate=pl.CostEstimate(flops=0, bytes_accessed=1024, transcendentals=0),
    )(table, own_c, *operands)


def flatten_kernel(tile, out):
    out[0] = tile[0, 0, 0].reshape(BS, WIDE)


def flatten(integrals, chunk):
    return pl.pallas_call(
        flatten_kernel,
        grid=(PER,),
        out_shape=jax.ShapeDtypeStruct((PER, BS, WIDE), jnp.bfloat16),
        in_specs=[pl.BlockSpec((1, 1, 1, BS, AB, BS), lambda b: (0, 0, chunk * PER + b, 0, 0, 0))],
        out_specs=pl.BlockSpec((1, BS, WIDE), lambda b: (b, 0, 0)),
        cost_estimate=pl.CostEstimate(flops=0, bytes_accessed=8 * 1024 * 1024, transcendentals=0),
    )(integrals)


def per_device(integrals, block_list, pair_count, occupied, virtual):
    own_c = occupied[0]
    ao = lax.axis_index("ao")
    aux = lax.axis_index("aux")
    where = jnp.stack([ao, aux]).astype(jnp.int32)

    own = [flatten(integrals, 0)]
    lists = jnp.concatenate([block_list.reshape(1, 32), pair_count], axis=1)
    own[0], lists = lax.optimization_barrier((own[0], lists))
    lists = jnp.concatenate([lists, around(lists, 1)], axis=0)
    integrals, lists = lax.optimization_barrier((integrals, lists))
    own.append(flatten(integrals, 1))
    lists = jnp.concatenate([lists, around(lists, 2)], axis=0)
    lists = lax.ppermute(lists, "aux", [(g, g ^ 1) for g in range(8)])
    lists = jnp.concatenate([lists, around(lists, 1)], axis=0)
    lists = jnp.concatenate([lists, around(lists, 2)], axis=0)
    table = plan(lists, where)
    longest = table[0]

    last = [across(own[c], 1) for c in range(CHUNKS)]
    following = [across(own[c], -1) for c in range(CHUNKS)]
    first, _, table = lax.optimization_barrier((last[0], following[0], table))
    far = [across(first, 1), across(following[1], -1)]
    tiles = [own, following, far, last]

    came = []

    def add(acc, near, some):
        blocks = [chunk for tile in near for chunk in tiles[tile]] + [b for q in some for b in came[q]]
        return run(
            functools.partial(sum_kernel, near, some, acc is None), table, own_c,
            ([] if acc is None else [acc]) + blocks, (), 2 * SIDE + 2 * G * len(some), False,
        )

    acc = add(None, (0, 1, 3), ())
    table, acc, far[0] = lax.optimization_barrier((table, acc, far[0]))
    for q in range(ALWAYS):
        if q >= DELAY:
            acc = add(acc, (FAR,) if q == DELAY else (), (q - DELAY,))
            table, acc = lax.optimization_barrier((table, acc))
        up, down = pack(q, table, tiles, came)
        came.append(list(lax.optimization_barrier((around(up, 1), around(down, -1)))))
    acc = add(acc, (), (ALWAYS - 2,))

    block = virtual[0]
    zero = jnp.zeros_like(block)
    turn = jnp.concatenate(
        [jnp.concatenate([block, zero], axis=1), jnp.concatenate([zero, block], axis=1)], axis=0
    )

    def finish(some, came, acc, turn):
        return run(
            functools.partial(last_kernel, some), table, own_c,
            [acc, turn] + own + [b for q in some for b in came[q]], (1,), 2 * G * len(some), True,
        )

    def ending(extra):
        def branch(came, acc, turn):
            came = list(came)
            for q in range(ALWAYS, ALWAYS + extra):
                up, down = pack(q, table, tiles, came)
                came.append([around(up, 1), around(down, -1)])
            return finish(tuple(range(ALWAYS - 1, ALWAYS + extra)), came, acc, turn)
        return branch

    more = (longest > G * ALWAYS).astype(jnp.int32) + (longest > G * (ALWAYS + 1)).astype(jnp.int32)
    partial = lax.switch(more, [ending(extra) for extra in range(STEPS - ALWAYS + 1)], came, acc, turn)

    pieces = lax.all_to_all(partial.reshape(128, 2), AXES, split_axis=0, concat_axis=0, tiled=True)
    return pieces.sum(axis=0).reshape(1, 2)


def solution(mesh):
    placed = (
        P("ao", "aux", None, None, None, None),
        P("ao", None, None),
        P("ao", None),
        P("ao", None, None, None, None, None),
        P("aux", None, None),
    )
    return jax.shard_map(
        per_device, mesh=mesh, in_specs=placed, out_specs=P("ao", "aux"), check_vma=False
    )
```

```python
import functools

import jax
import jax.numpy as jnp
from jax import lax
from jax.experimental import pallas as pl
from jax.experimental.pallas import tpu as pltpu
from jax.sharding import PartitionSpec as P

BS = 128
NB = 8
AB = 16
WIDE = AB * BS
ROWS = NB * BS
AXES = ("ao", "aux")
SIDE = 4
N_AO = 16
LIST = 48
CHUNKS = 2
PER = NB // CHUNKS
G = 3
ALWAYS = 4
STEPS = 6
DELAY = 2
RELAY = 32
FIRST = G
FAR = 2
ORDER = (0, 1, 3, FAR)
PARTS = 4
SEND, TAKE, NEAR = 16, 64, 128
VMEM_BYTES = 56 * 1024 * 1024


def shift(ring, step):
    pairs = []
    for z in range(SIDE):
        for x in range(SIDE):
            for aux in range(8):
                along_x = (aux % 2 == 0) != ring
                to = z * SIDE + (x + step) % SIDE if along_x else (z + step) % SIDE * SIDE + x
                pairs.append(((z * SIDE + x) * 8 + aux, to * 8 + aux))
    return pairs


def across(array, step):
    return lax.ppermute(array, AXES, shift(False, step))


def around(array, step):
    return lax.ppermute(array, AXES, shift(True, step))


def index_of(core, t, e):
    return jnp.where(core == 0, t * SIDE + e, e * SIDE + t)


def pick(values, t):
    out = values[0]
    for s in range(1, SIDE):
        out = jnp.where(t == s, values[s], out)
    return out


def ring_plan(lists, core, e):
    def count(ts, td):
        td = index_of(core, td % SIDE, e)
        near = lists[index_of(core, ts, (e + ORDER[0]) % SIDE), 32 + td]
        for rel in ORDER[1:-1]:
            near = near + lists[index_of(core, ts, (e + rel) % SIDE), 32 + td]
        return near, near + lists[index_of(core, ts, (e + FAR) % SIDE), 32 + td]

    ones = [[count(t, t + step) for t in range(SIDE)] for step in (1, 3)]
    twos = [count(t, t + 2) for t in range(SIDE)]

    def layout(ups):
        ways = []
        for way, sender in ((0, 3), (1, 1)):
            two, two_near, gap, early, late, own, held_up = [], [], [], [], [], [], []
            for t in range(SIDE):
                if way == 0:
                    h = ups[t]
                    hn = jnp.minimum(h, twos[t][0])
                else:
                    h = twos[t][1] - ups[t]
                    hn = jnp.maximum(twos[t][0] - ups[t], 0)
                u = jnp.maximum(FIRST - hn, 0)
                us = jnp.minimum(u, ones[way][t][0])
                two.append(h)
                two_near.append(hn)
                gap.append(u)
                early.append(us)
                late.append(u + h)
                own.append(u + h + ones[way][t][1] - us)
                held_up.append(DELAY * G + jnp.where(h > hn, u, 0))
            relay = [jnp.maximum(own[t], held_up[(t + sender) % SIDE]) for t in range(SIDE)]
            length = [relay[t] + two[(t + sender) % SIDE] for t in range(SIDE)]
            ways.append(dict(two=two, two_near=two_near, gap=gap, early=early, late=late, relay=relay, length=length))
        return ways

    def longest(ups):
        up, down = layout(ups)
        return functools.reduce(jnp.maximum, up["length"] + down["length"])

    plain = [twos[t][1] // 2 for t in range(SIDE)]
    ups = list(plain)
    for _ in range(2):
        for t in range(SIDE):
            up, down = (way["length"] for way in layout(ups))
            excess = jnp.maximum(up[t], up[(t + 1) % SIDE]) - jnp.maximum(down[t], down[(t + 3) % SIDE])
            move = jnp.where(excess >= 0, excess // 2, -((-excess) // 2))
            ups[t] = jnp.clip(ups[t] - move, 0, twos[t][1])
    better = longest(ups) < longest(plain)
    ups = [jnp.where(better, a, b) for a, b in zip(ups, plain)]
    return ups, layout(ups), longest(ups)


def plan_kernel(came, where, table, lists):
    ao, aux = where[0], where[1]
    core = aux % 2
    z, x = ao // SIDE, ao % SIDE
    t = jnp.where(core == 0, z, x)
    e = jnp.where(core == 0, x, z)

    def place(r, _):
        i = index_of(core, (t - r // SIDE + SIDE) % SIDE, (e - r % SIDE + SIDE) % SIDE)
        for c in range(LIST):
            lists[i, c] = came[r, c]
        return 0

    lax.fori_loop(0, N_AO, place, 0)

    def ring(r, most):
        return jnp.maximum(most, ring_plan(lists, r // SIDE, r % SIDE)[2])

    table[0] = lax.fori_loop(0, 2 * SIDE, ring, jnp.int32(0))
    ups, ways, _ = ring_plan(lists, core, e)

    for r in range(G * STEPS):
        for way in range(2):
            table[SEND + 24 * way + r] = 0
            table[TAKE + 24 * way + r] = -1

    def each(ts, td, then):
        ts, td = ts % SIDE, td % SIDE
        d = index_of(core, td, e)
        n = jnp.int32(0)
        for rel in ORDER:
            i = index_of(core, ts, (e + rel) % SIDE)
            count = lists[i, 32 + d]
            for k in range(2):
                @pl.when(k < count)
                def _(n=n, i=i, k=k, rel=rel):
                    then(n, rel * NB + lists[i, 2 * d + k], 2 * i + k)
                n = n + jnp.where(k < count, 1, 0)
        return n

    def at_two(way, s, n):
        return n + jnp.where(n >= pick(way["two_near"], s), pick(way["gap"], s), 0)

    def at_one(way, s, n):
        early = pick(way["early"], s)
        return n + jnp.where(n < early, pick(way["two_near"], s), pick(way["late"], s) - early)

    my_up = pick(ups, t)

    def send_two(n, held, slot):
        @pl.when(n < my_up)
        def _():
            table[SEND + at_two(ways[0], t, n)] = held

        @pl.when(n >= my_up)
        def _():
            table[SEND + 24 + at_two(ways[1], t, n - my_up)] = held

    each(t, t + 2, send_two)
    opposite = (t + 2) % SIDE
    far_up = pick(ups, opposite)
    for way, step in ((0, 1), (1, 3)):
        sender = (t + 4 - step) % SIDE

        def send_one(n, held, slot, way=way):
            table[SEND + 24 * way + at_one(ways[way], t, n)] = held

        each(t, t + step, send_one)

        def relay(j, _, way=way, sender=sender):
            table[SEND + 24 * way + pick(ways[way]["relay"], t) + j] = RELAY + at_two(ways[way], sender, j)
            return 0

        lax.fori_loop(0, pick(ways[way]["two"], sender), relay, 0)

        def take_one(n, held, slot, way=way, sender=sender):
            table[TAKE + 24 * way + at_one(ways[way], sender, n)] = slot

        each(sender, t, take_one)

    def take_two(n, held, slot):
        @pl.when(n < far_up)
        def _():
            table[TAKE + pick(ways[0]["relay"], (t + 3) % SIDE) + n] = slot

        @pl.when(n >= far_up)
        def _():
            table[TAKE + 24 + pick(ways[1]["relay"], (t + 1) % SIDE) + n - far_up] = slot

    each(opposite, t, take_two)

    def near(n, held, slot):
        table[NEAR + n] = held * 32 + slot

    table[1] = each(t, t, near)


def plan(lists, where):
    smem = pl.BlockSpec(memory_space=pltpu.SMEM)
    return pl.pallas_call(
        plan_kernel,
        out_shape=jax.ShapeDtypeStruct((256,), jnp.int32),
        in_specs=[smem, smem],
        out_specs=smem,
        scratch_shapes=[pltpu.SMEM((N_AO, LIST), jnp.int32)],
    )(lists, where)


def pack_kernel(step, held, relays, table, *refs):
    refs = list(refs)
    tiles = {m: [refs.pop(0) for _ in range(CHUNKS)] for m in held}
    came = [refs.pop(0) for _ in range(2 * relays)]
    up, down, room, sems = refs
    arrivals, leavings = [], []
    for way, out in enumerate((up, down)):
        for h in range(G):
            k = G * way + h
            code = table[SEND + 24 * way + G * step + h]
            dst = room.at[k]

            @pl.when(code < RELAY)
            def _(code=code, dst=dst, k=k):
                for m in held:
                    for c, tile in enumerate(tiles[m]):
                        @pl.when(code // PER == m * CHUNKS + c)
                        def _():
                            pltpu.make_async_copy(tile.at[code % PER], dst, sems.at[k]).start()

            @pl.when(code >= RELAY)
            def _(code=code, dst=dst, k=k, way=way):
                for q in range(relays):
                    @pl.when((code - RELAY) // G == q)
                    def _():
                        pltpu.make_async_copy(came[2 * q + way].at[(code - RELAY) % G], dst, sems.at[k]).start()

            arrivals.append(pltpu.make_async_copy(tiles[0][0].at[0], dst, sems.at[k]))
            leavings.append(pltpu.make_async_copy(dst, out.at[h], sems.at[2 * G + k]))
    for arrival, leaving in zip(arrivals, leavings):
        arrival.wait()
        leaving.start()
    for leaving in leavings:
        leaving.wait()


def pack(step, table, tiles, came):
    relays = max(step - DELAY + 1, 0)
    held = [m for m in ORDER if G * step >= FIRST or m != FAR]
    smem = pl.BlockSpec(memory_space=pltpu.SMEM)
    hbm = pl.BlockSpec(memory_space=pl.ANY)
    operands = [chunk for m in held for chunk in tiles[m]]
    for q in range(relays):
        operands += came[q]
    shape = jax.ShapeDtypeStruct((G, BS, WIDE), jnp.bfloat16)
    return pl.pallas_call(
        functools.partial(pack_kernel, step, held, relays),
        out_shape=[shape, shape],
        in_specs=[smem] + [hbm] * len(operands),
        out_specs=[hbm, hbm],
        scratch_shapes=[pltpu.VMEM((2 * G, BS, WIDE), jnp.bfloat16), pltpu.SemaphoreType.DMA((4 * G,))],
        cost_estimate=pl.CostEstimate(flops=0, bytes_accessed=1024, transcendentals=0),
    )(table, *operands)


def gather(own_c, left, right, sems, wanted):
    n = jnp.int32(0)
    for ok, slot, start in wanted:
        @pl.when(ok)
        def _(n=n, slot=slot, start=start):
            at = pl.ds(pl.multiple_of(n * BS, BS), BS)
            pltpu.make_async_copy(own_c.at[:, slot // 2, slot % 2], left.at[:, :, at], sems.at[0]).start()
            start(right.at[at], sems.at[1])
        n = n + jnp.where(ok, 1, 0)
    return n


def arrive(own_c, left, right, sems, n):
    def one(_, carry):
        at = pl.ds(0, BS)
        pltpu.make_async_copy(own_c.at[:, 0, 0], left.at[:, :, at], sems.at[0]).wait()
        pltpu.make_async_copy(right.at[at], right.at[at], sems.at[1]).wait()
        return carry

    lax.fori_loop(0, n, one, 0)

    @pl.when(n % 2 == 1)
    def _():
        at = pl.ds(pl.multiple_of(n * BS, BS), BS)
        left[:, :, at] = jnp.zeros((NB, BS, BS), jnp.bfloat16)
        right[at, :] = jnp.zeros((BS, WIDE), jnp.bfloat16)


def contract(left, right, n, acc, cols):
    def pair(p, carry):
        at = pl.ds(pl.multiple_of(p * 2 * BS, 2 * BS), 2 * BS)
        acc[:, cols] += jnp.dot(
            left[:, :, at].reshape(ROWS, 2 * BS), right[at, cols], preferred_element_type=jnp.float32
        )
        return carry

    lax.fori_loop(0, (n + 1) // 2, pair, 0)


def from_steps(table, steps, came):
    wanted = []
    for q, step in enumerate(steps):
        for way in range(2):
            for h in range(G):
                slot = table[TAKE + 24 * way + G * step + h]

                def start(dst, sem, q=q, way=way, h=h):
                    pltpu.make_async_copy(came[2 * q + way].at[h], dst, sem).start()

                wanted.append((slot >= 0, jnp.maximum(slot, 0), start))
    return wanted


def sum_kernel(near, steps, clear, table, own_c, *refs):
    refs = list(refs)
    before = None if clear else refs.pop(0)
    tiles = {m: [refs.pop(0) for _ in range(CHUNKS)] for m in near}
    came = [refs.pop(0) for _ in range(2 * len(steps))]
    out, left, right, acc, sems = refs
    wanted = from_steps(table, steps, came)
    for s in range(2 * SIDE if near else 0):
        entry = table[NEAR + s]
        code = entry // 32
        here = jnp.bool_(False)
        for m in near:
            here = jnp.logical_or(here, code // NB == m)

        def start(dst, sem, code=code):
            for m in near:
                for c, chunk in enumerate(tiles[m]):
                    @pl.when(code // PER == m * CHUNKS + c)
                    def _():
                        pltpu.make_async_copy(chunk.at[code % PER], dst, sem).start()

        wanted.append((jnp.logical_and(s < table[1], here), entry % 32, start))
    n = gather(own_c, left, right, sems, wanted)
    parts = [slice(j * WIDE // PARTS, (j + 1) * WIDE // PARTS) for j in range(PARTS)]
    fetches = []
    for j, cols in enumerate(parts):
        if clear:
            acc[:, cols] = jnp.zeros((ROWS, WIDE // PARTS), jnp.float32)
        else:
            copy = pltpu.make_async_copy(before.at[:, cols], acc.at[:, cols], sems.at[2 + j])
            copy.start()
            fetches.append(copy)
    arrive(own_c, left, right, sems, n)
    stores = []
    for j, cols in enumerate(parts):
        if not clear:
            fetches[j].wait()
        contract(left, right, n, acc, cols)
        copy = pltpu.make_async_copy(acc.at[:, cols], out.at[:, cols], sems.at[2 + j])
        copy.start()
        stores.append(copy)
    for copy in stores:
        copy.wait()


def last_kernel(steps, table, own_c, before, turn, first, second, *refs):
    came = refs[:2 * len(steps)]
    out, left, right, acc, rows, part, mixed, total, sems = refs[2 * len(steps):]
    n = gather(own_c, left, right, sems, from_steps(table, steps, came))
    fetches = []
    for j in range(PARTS):
        cols = pl.ds(j * WIDE // PARTS, WIDE // PARTS)
        copy = pltpu.make_async_copy(before.at[:, cols], acc.at[:, cols], sems.at[2 + j])
        copy.start()
        fetches.append(copy)
    own = []
    for c, chunk in enumerate((first, second)):
        copy = pltpu.make_async_copy(chunk, rows.at[pl.ds(c * PER, PER)], sems.at[2 + PARTS + c])
        copy.start()
        own.append(copy)
    arrive(own_c, left, right, sems, n)
    pairs = (n + 1) // 2
    for j, fetch in enumerate(fetches):
        fetch.wait()
        cols = slice(j * WIDE // PARTS, (j + 1) * WIDE // PARTS)

        @pl.when(pairs == 0)
        def _():
            part[:, cols] = acc[:, cols].astype(jnp.bfloat16)

        for p in range(1, G * len(steps) + 1):
            @pl.when(pairs == p)
            def _():
                added = jnp.dot(
                    left[:, :, :2 * p * BS].reshape(ROWS, 2 * p * BS), right[:2 * p * BS, cols],
                    preferred_element_type=jnp.float32,
                )
                part[:, cols] = (acc[:, cols] + added).astype(jnp.bfloat16)

        for k in range(WIDE // PARTS // 256):
            here = slice(cols.start + k * 256, cols.start + (k + 1) * 256)
            mixed[:, here] = jnp.dot(
                part[:, here], turn[...], preferred_element_type=jnp.float32
            ).astype(jnp.bfloat16)

    for copy in own:
        copy.wait()
    total[...] = jnp.zeros_like(total)

    @pl.loop(0, ROWS // 32, unroll=4)
    def _(j):
        def stacked(load):
            halves = []
            for h in range(2):
                at = pl.multiple_of(j * 32 + h * 16, 16)
                halves.append(jnp.concatenate([load(at, slice(p * BS, (p + 1) * BS)) for p in range(AB)], axis=0))
            return jnp.concatenate(halves, axis=1)

        block = j // (BS // 32)
        total[...] += lax.dot_general(
            stacked(lambda at, cols: mixed[pl.ds(at, 16), cols]),
            stacked(lambda at, cols: rows[block, pl.ds(pl.multiple_of(at - block * BS, 16), 16), cols]),
            (((1,), (1,)), ((), ())),
            preferred_element_type=jnp.float32,
        )

    r = lax.broadcasted_iota(jnp.int32, (256, 256), 0)
    c = lax.broadcasted_iota(jnp.int32, (256, 256), 1)
    kept = jnp.where(r % 16 == c % 16, total[...], 0.0)
    kept = kept.reshape(16, 16, 256).sum(axis=1)
    rr = lax.broadcasted_iota(jnp.int32, (256, 16), 0)
    cc = lax.broadcasted_iota(jnp.int32, (256, 16), 1)
    pick_q = jnp.where(rr // 16 == cc, 1.0, 0.0)
    out[...] = jnp.dot(kept, pick_q, preferred_element_type=jnp.float32, precision=lax.Precision.HIGHEST)


def run(kernel, table, own_c, operands, vmem_operands, blocks, last):
    smem = pl.BlockSpec(memory_space=pltpu.SMEM)
    vmem = pl.BlockSpec(memory_space=pltpu.VMEM)
    hbm = pl.BlockSpec(memory_space=pl.ANY)
    scratch = [
        pltpu.VMEM((NB, BS, blocks * BS), jnp.bfloat16),
        pltpu.VMEM((blocks * BS, WIDE), jnp.bfloat16),
        pltpu.VMEM((ROWS, WIDE), jnp.float32),
    ]
    if last:
        scratch += [
            pltpu.VMEM((NB, BS, WIDE), jnp.bfloat16),
            pltpu.VMEM((ROWS, WIDE), jnp.bfloat16),
            pltpu.VMEM((ROWS, WIDE), jnp.bfloat16),
            pltpu.VMEM((256, 256), jnp.float32),
        ]
    scratch.append(pltpu.SemaphoreType.DMA((4 + PARTS,)))
    shape = (16, 16) if last else (ROWS, WIDE)
    return pl.pallas_call(
        kernel,
        out_shape=jax.ShapeDtypeStruct(shape, jnp.float32),
        in_specs=[smem, hbm] + [vmem if k in vmem_operands else hbm for k in range(len(operands))],
        out_specs=vmem if last else hbm,
        scratch_shapes=scratch,
        compiler_params=pltpu.CompilerParams(vmem_limit_bytes=VMEM_BYTES),
        cost_estimate=pl.CostEstimate(flops=0, bytes_accessed=1024, transcendentals=0),
    )(table, own_c, *operands)


def flatten_kernel(tile, out):
    out[0] = tile[0, 0, 0].reshape(BS, WIDE)


def flatten(integrals, chunk):
    return pl.pallas_call(
        flatten_kernel,
        grid=(PER,),
        out_shape=jax.ShapeDtypeStruct((PER, BS, WIDE), jnp.bfloat16),
        in_specs=[pl.BlockSpec((1, 1, 1, BS, AB, BS), lambda b: (0, 0, chunk * PER + b, 0, 0, 0))],
        out_specs=pl.BlockSpec((1, BS, WIDE), lambda b: (b, 0, 0)),
        cost_estimate=pl.CostEstimate(flops=0, bytes_accessed=8 * 1024 * 1024, transcendentals=0),
    )(integrals)


def per_device(integrals, block_list, pair_count, occupied, virtual):
    own_c = occupied[0]
    ao = lax.axis_index("ao")
    aux = lax.axis_index("aux")
    where = jnp.stack([ao, aux]).astype(jnp.int32)

    own = [flatten(integrals, 0)]
    lists = jnp.concatenate([block_list.reshape(1, 32), pair_count], axis=1)
    own[0], lists = lax.optimization_barrier((own[0], lists))
    lists = jnp.concatenate([lists, around(lists, 1)], axis=0)
    integrals, lists = lax.optimization_barrier((integrals, lists))
    own.append(flatten(integrals, 1))
    lists = jnp.concatenate([lists, around(lists, 2)], axis=0)
    lists = lax.ppermute(lists, "aux", [(g, g ^ 1) for g in range(8)])
    lists = jnp.concatenate([lists, around(lists, 1)], axis=0)
    lists = jnp.concatenate([lists, around(lists, 2)], axis=0)
    table = plan(lists, where)
    longest = table[0]

    last = [across(own[c], 1) for c in range(CHUNKS)]
    following = [across(own[c], -1) for c in range(CHUNKS)]
    first, _, table = lax.optimization_barrier((last[0], following[0], table))
    far = [across(first, 1), across(following[1], -1)]
    tiles = [own, following, far, last]

    came = []

    def add(acc, near, some):
        blocks = [chunk for tile in near for chunk in tiles[tile]] + [b for q in some for b in came[q]]
        return run(
            functools.partial(sum_kernel, near, some, acc is None), table, own_c,
            ([] if acc is None else [acc]) + blocks, (), 2 * SIDE + 2 * G * len(some), False,
        )

    acc = add(None, (0, 1, 3), ())
    table, acc, far[0] = lax.optimization_barrier((table, acc, far[0]))
    for q in range(ALWAYS):
        up, down = pack(q, table, tiles, came)
        if q == ALWAYS - 1:
            up, down, acc = lax.optimization_barrier((up, down, acc))
            acc = add(acc, (FAR,), tuple(range(q - 1)))
        came.append(list(lax.optimization_barrier((around(up, 1), around(down, -1)))))
    acc = add(acc, (), (ALWAYS - 2,))

    block = virtual[0]
    zero = jnp.zeros_like(block)
    turn = jnp.concatenate(
        [jnp.concatenate([block, zero], axis=1), jnp.concatenate([zero, block], axis=1)], axis=0
    )

    def finish(some, came, acc, turn):
        return run(
            functools.partial(last_kernel, some), table, own_c,
            [acc, turn] + own + [b for q in some for b in came[q]], (1,), 2 * G * len(some), True,
        )

    def ending(extra):
        def branch(came, acc, turn):
            came = list(came)
            for q in range(ALWAYS, ALWAYS + extra):
                up, down = pack(q, table, tiles, came)
                came.append([around(up, 1), around(down, -1)])
            return finish(tuple(range(ALWAYS - 1, ALWAYS + extra)), came, acc, turn)
        return branch

    more = (longest > G * ALWAYS).astype(jnp.int32) + (longest > G * (ALWAYS + 1)).astype(jnp.int32)
    partial = lax.switch(more, [ending(extra) for extra in range(STEPS - ALWAYS + 1)], came, acc, turn)

    pieces = lax.all_to_all(partial.reshape(128, 2), AXES, split_axis=0, concat_axis=0, tiled=True)
    return pieces.sum(axis=0).reshape(1, 2)


def solution(mesh):
    placed = (
        P("ao", "aux", None, None, None, None),
        P("ao", None, None),
        P("ao", None),
        P("ao", None, None, None, None, None),
        P("aux", None, None),
    )
    return jax.shard_map(
        per_device, mesh=mesh, in_specs=placed, out_specs=P("ao", "aux"), check_vma=False
    )
```

```python
import functools

import jax
import jax.numpy as jnp
from jax import lax
from jax.experimental import pallas as pl
from jax.experimental.pallas import tpu as pltpu
from jax.sharding import PartitionSpec as P

BS = 128
NB = 8
AB = 16
WIDE = AB * BS
ROWS = NB * BS
AXES = ("ao", "aux")
SIDE = 4
N_AO = 16
LIST = 48
CHUNKS = 2
PER = NB // CHUNKS
G = 3
ALWAYS = 4
STEPS = 6
DELAY = 2
RELAY = 32
FIRST = G
FAR = 2
ORDER = (0, 1, 3, FAR)
PARTS = 4
SEND, TAKE, NEAR = 16, 64, 128
VMEM_BYTES = 56 * 1024 * 1024


def shift(ring, step):
    pairs = []
    for z in range(SIDE):
        for x in range(SIDE):
            for aux in range(8):
                along_x = (aux % 2 == 0) != ring
                to = z * SIDE + (x + step) % SIDE if along_x else (z + step) % SIDE * SIDE + x
                pairs.append(((z * SIDE + x) * 8 + aux, to * 8 + aux))
    return pairs


def across(array, step):
    return lax.ppermute(array, AXES, shift(False, step))


def around(array, step):
    return lax.ppermute(array, AXES, shift(True, step))


def index_of(core, t, e):
    return jnp.where(core == 0, t * SIDE + e, e * SIDE + t)


def pick(values, t):
    out = values[0]
    for s in range(1, SIDE):
        out = jnp.where(t == s, values[s], out)
    return out


def ring_plan(lists, core, e):
    def count(ts, td):
        td = index_of(core, td % SIDE, e)
        near = lists[index_of(core, ts, (e + ORDER[0]) % SIDE), 32 + td]
        for rel in ORDER[1:-1]:
            near = near + lists[index_of(core, ts, (e + rel) % SIDE), 32 + td]
        return near, near + lists[index_of(core, ts, (e + FAR) % SIDE), 32 + td]

    ones = [[count(t, t + step) for t in range(SIDE)] for step in (1, 3)]
    twos = [count(t, t + 2) for t in range(SIDE)]

    def layout(ups):
        ways = []
        for way, sender in ((0, 3), (1, 1)):
            two, two_near, gap, early, late, own, held_up = [], [], [], [], [], [], []
            for t in range(SIDE):
                if way == 0:
                    h = ups[t]
                    hn = jnp.minimum(h, twos[t][0])
                else:
                    h = twos[t][1] - ups[t]
                    hn = jnp.maximum(twos[t][0] - ups[t], 0)
                u = jnp.maximum(FIRST - hn, 0)
                us = jnp.minimum(u, ones[way][t][0])
                two.append(h)
                two_near.append(hn)
                gap.append(u)
                early.append(us)
                late.append(u + h)
                own.append(u + h + ones[way][t][1] - us)
                held_up.append(DELAY * G + jnp.where(h > hn, u, 0))
            relay = [jnp.maximum(own[t], held_up[(t + sender) % SIDE]) for t in range(SIDE)]
            length = [relay[t] + two[(t + sender) % SIDE] for t in range(SIDE)]
            ways.append(dict(two=two, two_near=two_near, gap=gap, early=early, late=late, relay=relay, length=length))
        return ways

    def longest(ups):
        up, down = layout(ups)
        return functools.reduce(jnp.maximum, up["length"] + down["length"])

    plain = [twos[t][1] // 2 for t in range(SIDE)]
    ups = list(plain)
    for _ in range(2):
        for t in range(SIDE):
            up, down = (way["length"] for way in layout(ups))
            excess = jnp.maximum(up[t], up[(t + 1) % SIDE]) - jnp.maximum(down[t], down[(t + 3) % SIDE])
            move = jnp.where(excess >= 0, excess // 2, -((-excess) // 2))
            ups[t] = jnp.clip(ups[t] - move, 0, twos[t][1])
    better = longest(ups) < longest(plain)
    ups = [jnp.where(better, a, b) for a, b in zip(ups, plain)]
    return ups, layout(ups), longest(ups)


def plan_kernel(came, where, table, lists):
    ao, aux = where[0], where[1]
    core = aux % 2
    z, x = ao // SIDE, ao % SIDE
    t = jnp.where(core == 0, z, x)
    e = jnp.where(core == 0, x, z)

    def place(r, _):
        i = index_of(core, (t - r // SIDE + SIDE) % SIDE, (e - r % SIDE + SIDE) % SIDE)
        for c in range(LIST):
            lists[i, c] = came[r, c]
        return 0

    lax.fori_loop(0, N_AO, place, 0)

    def ring(r, most):
        return jnp.maximum(most, ring_plan(lists, r // SIDE, r % SIDE)[2])

    table[0] = lax.fori_loop(0, 2 * SIDE, ring, jnp.int32(0))
    ups, ways, _ = ring_plan(lists, core, e)

    for r in range(G * STEPS):
        for way in range(2):
            table[SEND + 24 * way + r] = 0
            table[TAKE + 24 * way + r] = -1

    def each(ts, td, then):
        ts, td = ts % SIDE, td % SIDE
        d = index_of(core, td, e)
        n = jnp.int32(0)
        for rel in ORDER:
            i = index_of(core, ts, (e + rel) % SIDE)
            count = lists[i, 32 + d]
            for k in range(2):
                @pl.when(k < count)
                def _(n=n, i=i, k=k, rel=rel):
                    then(n, rel * NB + lists[i, 2 * d + k], 2 * i + k)
                n = n + jnp.where(k < count, 1, 0)
        return n

    def at_two(way, s, n):
        return n + jnp.where(n >= pick(way["two_near"], s), pick(way["gap"], s), 0)

    def at_one(way, s, n):
        early = pick(way["early"], s)
        return n + jnp.where(n < early, pick(way["two_near"], s), pick(way["late"], s) - early)

    my_up = pick(ups, t)

    def send_two(n, held, slot):
        @pl.when(n < my_up)
        def _():
            table[SEND + at_two(ways[0], t, n)] = held

        @pl.when(n >= my_up)
        def _():
            table[SEND + 24 + at_two(ways[1], t, n - my_up)] = held

    each(t, t + 2, send_two)
    opposite = (t + 2) % SIDE
    far_up = pick(ups, opposite)
    for way, step in ((0, 1), (1, 3)):
        sender = (t + 4 - step) % SIDE

        def send_one(n, held, slot, way=way):
            table[SEND + 24 * way + at_one(ways[way], t, n)] = held

        each(t, t + step, send_one)

        def relay(j, _, way=way, sender=sender):
            table[SEND + 24 * way + pick(ways[way]["relay"], t) + j] = RELAY + at_two(ways[way], sender, j)
            return 0

        lax.fori_loop(0, pick(ways[way]["two"], sender), relay, 0)

        def take_one(n, held, slot, way=way, sender=sender):
            table[TAKE + 24 * way + at_one(ways[way], sender, n)] = slot

        each(sender, t, take_one)

    def take_two(n, held, slot):
        @pl.when(n < far_up)
        def _():
            table[TAKE + pick(ways[0]["relay"], (t + 3) % SIDE) + n] = slot

        @pl.when(n >= far_up)
        def _():
            table[TAKE + 24 + pick(ways[1]["relay"], (t + 1) % SIDE) + n - far_up] = slot

    each(opposite, t, take_two)

    def near(n, held, slot):
        table[NEAR + n] = held * 32 + slot

    table[1] = each(t, t, near)


def plan(lists, where):
    smem = pl.BlockSpec(memory_space=pltpu.SMEM)
    return pl.pallas_call(
        plan_kernel,
        out_shape=jax.ShapeDtypeStruct((256,), jnp.int32),
        in_specs=[smem, smem],
        out_specs=smem,
        scratch_shapes=[pltpu.SMEM((N_AO, LIST), jnp.int32)],
    )(lists, where)


def pack_kernel(step, held, relays, table, *refs):
    refs = list(refs)
    tiles = {m: [refs.pop(0) for _ in range(CHUNKS)] for m in held}
    came = [refs.pop(0) for _ in range(2 * relays)]
    up, down, room, sems = refs
    arrivals, leavings = [], []
    for way, out in enumerate((up, down)):
        for h in range(G):
            k = G * way + h
            code = table[SEND + 24 * way + G * step + h]
            dst = room.at[k]

            @pl.when(code < RELAY)
            def _(code=code, dst=dst, k=k):
                for m in held:
                    for c, tile in enumerate(tiles[m]):
                        @pl.when(code // PER == m * CHUNKS + c)
                        def _():
                            pltpu.make_async_copy(tile.at[code % PER], dst, sems.at[k]).start()

            @pl.when(code >= RELAY)
            def _(code=code, dst=dst, k=k, way=way):
                for q in range(relays):
                    @pl.when((code - RELAY) // G == q)
                    def _():
                        pltpu.make_async_copy(came[2 * q + way].at[(code - RELAY) % G], dst, sems.at[k]).start()

            arrivals.append(pltpu.make_async_copy(tiles[0][0].at[0], dst, sems.at[k]))
            leavings.append(pltpu.make_async_copy(dst, out.at[h], sems.at[2 * G + k]))
    for arrival, leaving in zip(arrivals, leavings):
        arrival.wait()
        leaving.start()
    for leaving in leavings:
        leaving.wait()


def pack(step, table, tiles, came):
    relays = max(step - DELAY + 1, 0)
    held = [m for m in ORDER if G * step >= FIRST or m != FAR]
    smem = pl.BlockSpec(memory_space=pltpu.SMEM)
    hbm = pl.BlockSpec(memory_space=pl.ANY)
    operands = [chunk for m in held for chunk in tiles[m]]
    for q in range(relays):
        operands += came[q]
    shape = jax.ShapeDtypeStruct((G, BS, WIDE), jnp.bfloat16)
    return pl.pallas_call(
        functools.partial(pack_kernel, step, held, relays),
        out_shape=[shape, shape],
        in_specs=[smem] + [hbm] * len(operands),
        out_specs=[hbm, hbm],
        scratch_shapes=[pltpu.VMEM((2 * G, BS, WIDE), jnp.bfloat16), pltpu.SemaphoreType.DMA((4 * G,))],
        cost_estimate=pl.CostEstimate(flops=0, bytes_accessed=1024, transcendentals=0),
    )(table, *operands)


def gather(own_c, left, right, sems, wanted):
    n = jnp.int32(0)
    for ok, slot, start in wanted:
        @pl.when(ok)
        def _(n=n, slot=slot, start=start):
            at = pl.ds(pl.multiple_of(n * BS, BS), BS)
            pltpu.make_async_copy(own_c.at[:, slot // 2, slot % 2], left.at[:, :, at], sems.at[0]).start()
            start(right.at[at], sems.at[1])
        n = n + jnp.where(ok, 1, 0)
    return n


def arrive(own_c, left, right, sems, n):
    def one(_, carry):
        at = pl.ds(0, BS)
        pltpu.make_async_copy(own_c.at[:, 0, 0], left.at[:, :, at], sems.at[0]).wait()
        pltpu.make_async_copy(right.at[at], right.at[at], sems.at[1]).wait()
        return carry

    lax.fori_loop(0, n, one, 0)

    @pl.when(n % 2 == 1)
    def _():
        at = pl.ds(pl.multiple_of(n * BS, BS), BS)
        left[:, :, at] = jnp.zeros((NB, BS, BS), jnp.bfloat16)
        right[at, :] = jnp.zeros((BS, WIDE), jnp.bfloat16)


def contract(left, right, n, acc, cols):
    def pair(p, carry):
        at = pl.ds(pl.multiple_of(p * 2 * BS, 2 * BS), 2 * BS)
        acc[:, cols] += jnp.dot(
            left[:, :, at].reshape(ROWS, 2 * BS), right[at, cols], preferred_element_type=jnp.float32
        )
        return carry

    lax.fori_loop(0, (n + 1) // 2, pair, 0)


def from_steps(table, steps, came):
    wanted = []
    for q, step in enumerate(steps):
        for way in range(2):
            for h in range(G):
                slot = table[TAKE + 24 * way + G * step + h]

                def start(dst, sem, q=q, way=way, h=h):
                    pltpu.make_async_copy(came[2 * q + way].at[h], dst, sem).start()

                wanted.append((slot >= 0, jnp.maximum(slot, 0), start))
    return wanted


def sum_kernel(near, steps, clear, table, own_c, *refs):
    refs = list(refs)
    before = None if clear else refs.pop(0)
    tiles = {m: [refs.pop(0) for _ in range(CHUNKS)] for m in near}
    came = [refs.pop(0) for _ in range(2 * len(steps))]
    out, left, right, acc, sems = refs
    wanted = from_steps(table, steps, came)
    for s in range(2 * SIDE if near else 0):
        entry = table[NEAR + s]
        code = entry // 32
        here = jnp.bool_(False)
        for m in near:
            here = jnp.logical_or(here, code // NB == m)

        def start(dst, sem, code=code):
            for m in near:
                for c, chunk in enumerate(tiles[m]):
                    @pl.when(code // PER == m * CHUNKS + c)
                    def _():
                        pltpu.make_async_copy(chunk.at[code % PER], dst, sem).start()

        wanted.append((jnp.logical_and(s < table[1], here), entry % 32, start))
    n = gather(own_c, left, right, sems, wanted)
    parts = [slice(j * WIDE // PARTS, (j + 1) * WIDE // PARTS) for j in range(PARTS)]
    fetches = []
    for j, cols in enumerate(parts):
        if clear:
            acc[:, cols] = jnp.zeros((ROWS, WIDE // PARTS), jnp.float32)
        else:
            copy = pltpu.make_async_copy(before.at[:, cols], acc.at[:, cols], sems.at[2 + j])
            copy.start()
            fetches.append(copy)
    arrive(own_c, left, right, sems, n)
    stores = []
    for j, cols in enumerate(parts):
        if not clear:
            fetches[j].wait()
        contract(left, right, n, acc, cols)
        copy = pltpu.make_async_copy(acc.at[:, cols], out.at[:, cols], sems.at[2 + j])
        copy.start()
        stores.append(copy)
    for copy in stores:
        copy.wait()


def last_kernel(steps, table, own_c, before, turn, first, second, *refs):
    came = refs[:2 * len(steps)]
    out, left, right, acc, rows, part, mixed, total, sems = refs[2 * len(steps):]
    n = gather(own_c, left, right, sems, from_steps(table, steps, came))
    fetches = []
    for j in range(PARTS):
        cols = pl.ds(j * WIDE // PARTS, WIDE // PARTS)
        copy = pltpu.make_async_copy(before.at[:, cols], acc.at[:, cols], sems.at[2 + j])
        copy.start()
        fetches.append(copy)
    own = []
    for c, chunk in enumerate((first, second)):
        copy = pltpu.make_async_copy(chunk, rows.at[pl.ds(c * PER, PER)], sems.at[2 + PARTS + c])
        copy.start()
        own.append(copy)
    arrive(own_c, left, right, sems, n)
    pairs = (n + 1) // 2
    for j, fetch in enumerate(fetches):
        fetch.wait()
        cols = slice(j * WIDE // PARTS, (j + 1) * WIDE // PARTS)

        @pl.when(pairs == 0)
        def _():
            part[:, cols] = acc[:, cols].astype(jnp.bfloat16)

        for p in range(1, G * len(steps) + 1):
            @pl.when(pairs == p)
            def _():
                added = jnp.dot(
                    left[:, :, :2 * p * BS].reshape(ROWS, 2 * p * BS), right[:2 * p * BS, cols],
                    preferred_element_type=jnp.float32,
                )
                part[:, cols] = (acc[:, cols] + added).astype(jnp.bfloat16)

        for k in range(WIDE // PARTS // 256):
            here = slice(cols.start + k * 256, cols.start + (k + 1) * 256)
            mixed[:, here] = jnp.dot(
                part[:, here], turn[...], preferred_element_type=jnp.float32
            ).astype(jnp.bfloat16)

    for copy in own:
        copy.wait()
    total[...] = jnp.zeros_like(total)

    @pl.loop(0, ROWS // 32, unroll=4)
    def _(j):
        def stacked(load):
            halves = []
            for h in range(2):
                at = pl.multiple_of(j * 32 + h * 16, 16)
                halves.append(jnp.concatenate([load(at, slice(p * BS, (p + 1) * BS)) for p in range(AB)], axis=0))
            return jnp.concatenate(halves, axis=1)

        block = j // (BS // 32)
        total[...] += lax.dot_general(
            stacked(lambda at, cols: mixed[pl.ds(at, 16), cols]),
            stacked(lambda at, cols: rows[block, pl.ds(pl.multiple_of(at - block * BS, 16), 16), cols]),
            (((1,), (1,)), ((), ())),
            preferred_element_type=jnp.float32,
        )

    r = lax.broadcasted_iota(jnp.int32, (256, 256), 0)
    c = lax.broadcasted_iota(jnp.int32, (256, 256), 1)
    kept = jnp.where(r % 16 == c % 16, total[...], 0.0)
    kept = kept.reshape(16, 16, 256).sum(axis=1)
    rr = lax.broadcasted_iota(jnp.int32, (256, 16), 0)
    cc = lax.broadcasted_iota(jnp.int32, (256, 16), 1)
    pick_q = jnp.where(rr // 16 == cc, 1.0, 0.0)
    out[...] = jnp.dot(kept, pick_q, preferred_element_type=jnp.float32, precision=lax.Precision.HIGHEST)


def run(kernel, table, own_c, operands, vmem_operands, blocks, last):
    smem = pl.BlockSpec(memory_space=pltpu.SMEM)
    vmem = pl.BlockSpec(memory_space=pltpu.VMEM)
    hbm = pl.BlockSpec(memory_space=pl.ANY)
    scratch = [
        pltpu.VMEM((NB, BS, blocks * BS), jnp.bfloat16),
        pltpu.VMEM((blocks * BS, WIDE), jnp.bfloat16),
        pltpu.VMEM((ROWS, WIDE), jnp.float32),
    ]
    if last:
        scratch += [
            pltpu.VMEM((NB, BS, WIDE), jnp.bfloat16),
            pltpu.VMEM((ROWS, WIDE), jnp.bfloat16),
            pltpu.VMEM((ROWS, WIDE), jnp.bfloat16),
            pltpu.VMEM((256, 256), jnp.float32),
        ]
    scratch.append(pltpu.SemaphoreType.DMA((4 + PARTS,)))
    shape = (16, 16) if last else (ROWS, WIDE)
    return pl.pallas_call(
        kernel,
        out_shape=jax.ShapeDtypeStruct(shape, jnp.float32),
        in_specs=[smem, hbm] + [vmem if k in vmem_operands else hbm for k in range(len(operands))],
        out_specs=vmem if last else hbm,
        scratch_shapes=scratch,
        compiler_params=pltpu.CompilerParams(vmem_limit_bytes=VMEM_BYTES),
        cost_estimate=pl.CostEstimate(flops=0, bytes_accessed=1024, transcendentals=0),
    )(table, own_c, *operands)


def flatten_kernel(tile, out):
    out[0] = tile[0, 0, 0].reshape(BS, WIDE)


def flatten(integrals, chunk):
    return pl.pallas_call(
        flatten_kernel,
        grid=(PER,),
        out_shape=jax.ShapeDtypeStruct((PER, BS, WIDE), jnp.bfloat16),
        in_specs=[pl.BlockSpec((1, 1, 1, BS, AB, BS), lambda b: (0, 0, chunk * PER + b, 0, 0, 0))],
        out_specs=pl.BlockSpec((1, BS, WIDE), lambda b: (b, 0, 0)),
        cost_estimate=pl.CostEstimate(flops=0, bytes_accessed=8 * 1024 * 1024, transcendentals=0),
    )(integrals)


def per_device(integrals, block_list, pair_count, occupied, virtual):
    own_c = occupied[0]
    ao = lax.axis_index("ao")
    aux = lax.axis_index("aux")
    where = jnp.stack([ao, aux]).astype(jnp.int32)

    own = [flatten(integrals, 0)]
    lists = jnp.concatenate([block_list.reshape(1, 32), pair_count], axis=1)
    own[0], lists = lax.optimization_barrier((own[0], lists))
    lists = jnp.concatenate([lists, around(lists, 1)], axis=0)
    integrals, lists = lax.optimization_barrier((integrals, lists))
    own.append(flatten(integrals, 1))
    lists = jnp.concatenate([lists, around(lists, 2)], axis=0)
    lists = lax.ppermute(lists, "aux", [(g, g ^ 1) for g in range(8)])
    lists = jnp.concatenate([lists, around(lists, 1)], axis=0)
    lists = jnp.concatenate([lists, around(lists, 2)], axis=0)
    table = plan(lists, where)
    longest = table[0]

    last = [across(own[c], 1) for c in range(CHUNKS)]
    following = [across(own[c], -1) for c in range(CHUNKS)]
    first, _, table = lax.optimization_barrier((last[0], following[0], table))
    far = [across(first, 1), across(following[1], -1)]
    tiles = [own, following, far, last]

    came = []

    def add(acc, near, some):
        blocks = [chunk for tile in near for chunk in tiles[tile]] + [b for q in some for b in came[q]]
        return run(
            functools.partial(sum_kernel, near, some, acc is None), table, own_c,
            ([] if acc is None else [acc]) + blocks, (), 2 * SIDE + 2 * G * len(some), False,
        )

    acc = add(None, (0, 1, 3), ())
    table, acc = lax.optimization_barrier((table, acc))
    for q in range(ALWAYS):
        up, down = pack(q, table, tiles, came)
        if q == 0:
            up, down, table, far[0] = lax.optimization_barrier((up, down, table, far[0]))
        if q == ALWAYS - 1:
            up, down, acc = lax.optimization_barrier((up, down, acc))
            acc = add(acc, (FAR,), tuple(range(q - 1)))
        came.append(list(lax.optimization_barrier((around(up, 1), around(down, -1)))))
    acc = add(acc, (), (ALWAYS - 2,))

    block = virtual[0]
    zero = jnp.zeros_like(block)
    turn = jnp.concatenate(
        [jnp.concatenate([block, zero], axis=1), jnp.concatenate([zero, block], axis=1)], axis=0
    )

    def finish(some, came, acc, turn):
        return run(
            functools.partial(last_kernel, some), table, own_c,
            [acc, turn] + own + [b for q in some for b in came[q]], (1,), 2 * G * len(some), True,
        )

    def ending(extra):
        def branch(came, acc, turn):
            came = list(came)
            for q in range(ALWAYS, ALWAYS + extra):
                up, down = pack(q, table, tiles, came)
                came.append([around(up, 1), around(down, -1)])
            return finish(tuple(range(ALWAYS - 1, ALWAYS + extra)), came, acc, turn)
        return branch

    more = (longest > G * ALWAYS).astype(jnp.int32) + (longest > G * (ALWAYS + 1)).astype(jnp.int32)
    partial = lax.switch(more, [ending(extra) for extra in range(STEPS - ALWAYS + 1)], came, acc, turn)

    pieces = lax.all_to_all(partial.reshape(128, 2), AXES, split_axis=0, concat_axis=0, tiled=True)
    return pieces.sum(axis=0).reshape(1, 2)


def solution(mesh):
    placed = (
        P("ao", "aux", None, None, None, None),
        P("ao", None, None),
        P("ao", None),
        P("ao", None, None, None, None, None),
        P("aux", None, None),
    )
    return jax.shard_map(
        per_device, mesh=mesh, in_specs=placed, out_specs=P("ao", "aux"), check_vma=False
    )
```

```python
import functools

import jax
import jax.numpy as jnp
from jax import lax
from jax.experimental import pallas as pl
from jax.experimental.pallas import tpu as pltpu
from jax.sharding import PartitionSpec as P

BS = 128
NB = 8
AB = 16
WIDE = AB * BS
ROWS = NB * BS
AXES = ("ao", "aux")
SIDE = 4
N_AO = 16
LIST = 48
CHUNKS = 2
PER = NB // CHUNKS
G = 3
ALWAYS = 4
STEPS = 6
DELAY = 2
RELAY = 32
FIRST = G
FAR = 2
ORDER = (0, 1, 3, FAR)
PARTS = 4
SEND, TAKE, NEAR = 16, 64, 128
VMEM_BYTES = 56 * 1024 * 1024


def shift(ring, step):
    pairs = []
    for z in range(SIDE):
        for x in range(SIDE):
            for aux in range(8):
                along_x = (aux % 2 == 0) != ring
                to = z * SIDE + (x + step) % SIDE if along_x else (z + step) % SIDE * SIDE + x
                pairs.append(((z * SIDE + x) * 8 + aux, to * 8 + aux))
    return pairs


def across(array, step):
    return lax.ppermute(array, AXES, shift(False, step))


def around(array, step):
    return lax.ppermute(array, AXES, shift(True, step))


def index_of(core, t, e):
    return jnp.where(core == 0, t * SIDE + e, e * SIDE + t)


def pick(values, t):
    out = values[0]
    for s in range(1, SIDE):
        out = jnp.where(t == s, values[s], out)
    return out


def ring_plan(lists, core, e):
    def count(ts, td):
        td = index_of(core, td % SIDE, e)
        near = lists[index_of(core, ts, (e + ORDER[0]) % SIDE), 32 + td]
        for rel in ORDER[1:-1]:
            near = near + lists[index_of(core, ts, (e + rel) % SIDE), 32 + td]
        return near, near + lists[index_of(core, ts, (e + FAR) % SIDE), 32 + td]

    ones = [[count(t, t + step) for t in range(SIDE)] for step in (1, 3)]
    twos = [count(t, t + 2) for t in range(SIDE)]

    def layout(ups):
        ways = []
        for way, sender in ((0, 3), (1, 1)):
            two, two_near, gap, early, late, own, held_up = [], [], [], [], [], [], []
            for t in range(SIDE):
                if way == 0:
                    h = ups[t]
                    hn = jnp.minimum(h, twos[t][0])
                else:
                    h = twos[t][1] - ups[t]
                    hn = jnp.maximum(twos[t][0] - ups[t], 0)
                u = jnp.maximum(FIRST - hn, 0)
                us = jnp.minimum(u, ones[way][t][0])
                two.append(h)
                two_near.append(hn)
                gap.append(u)
                early.append(us)
                late.append(u + h)
                own.append(u + h + ones[way][t][1] - us)
                held_up.append(DELAY * G + jnp.where(h > hn, u, 0))
            relay = [jnp.maximum(own[t], held_up[(t + sender) % SIDE]) for t in range(SIDE)]
            length = [relay[t] + two[(t + sender) % SIDE] for t in range(SIDE)]
            ways.append(dict(two=two, two_near=two_near, gap=gap, early=early, late=late, relay=relay, length=length))
        return ways

    def longest(ups):
        up, down = layout(ups)
        return functools.reduce(jnp.maximum, up["length"] + down["length"])

    plain = [twos[t][1] // 2 for t in range(SIDE)]
    ups = list(plain)
    for _ in range(2):
        for t in range(SIDE):
            up, down = (way["length"] for way in layout(ups))
            excess = jnp.maximum(up[t], up[(t + 1) % SIDE]) - jnp.maximum(down[t], down[(t + 3) % SIDE])
            move = jnp.where(excess >= 0, excess // 2, -((-excess) // 2))
            ups[t] = jnp.clip(ups[t] - move, 0, twos[t][1])
    better = longest(ups) < longest(plain)
    ups = [jnp.where(better, a, b) for a, b in zip(ups, plain)]
    return ups, layout(ups), longest(ups)


def plan_kernel(came, where, table, lists):
    ao, aux = where[0], where[1]
    core = aux % 2
    z, x = ao // SIDE, ao % SIDE
    t = jnp.where(core == 0, z, x)
    e = jnp.where(core == 0, x, z)

    def place(r, _):
        i = index_of(core, (t - r // SIDE + SIDE) % SIDE, (e - r % SIDE + SIDE) % SIDE)
        for c in range(LIST):
            lists[i, c] = came[r, c]
        return 0

    lax.fori_loop(0, N_AO, place, 0)

    def ring(r, most):
        return jnp.maximum(most, ring_plan(lists, r // SIDE, r % SIDE)[2])

    table[0] = lax.fori_loop(0, 2 * SIDE, ring, jnp.int32(0))
    ups, ways, _ = ring_plan(lists, core, e)

    for r in range(G * STEPS):
        for way in range(2):
            table[SEND + 24 * way + r] = 0
            table[TAKE + 24 * way + r] = -1

    def each(ts, td, then):
        ts, td = ts % SIDE, td % SIDE
        d = index_of(core, td, e)
        n = jnp.int32(0)
        for rel in ORDER:
            i = index_of(core, ts, (e + rel) % SIDE)
            count = lists[i, 32 + d]
            for k in range(2):
                @pl.when(k < count)
                def _(n=n, i=i, k=k, rel=rel):
                    then(n, rel * NB + lists[i, 2 * d + k], 2 * i + k)
                n = n + jnp.where(k < count, 1, 0)
        return n

    def at_two(way, s, n):
        return n + jnp.where(n >= pick(way["two_near"], s), pick(way["gap"], s), 0)

    def at_one(way, s, n):
        early = pick(way["early"], s)
        return n + jnp.where(n < early, pick(way["two_near"], s), pick(way["late"], s) - early)

    my_up = pick(ups, t)

    def send_two(n, held, slot):
        @pl.when(n < my_up)
        def _():
            table[SEND + at_two(ways[0], t, n)] = held

        @pl.when(n >= my_up)
        def _():
            table[SEND + 24 + at_two(ways[1], t, n - my_up)] = held

    each(t, t + 2, send_two)
    opposite = (t + 2) % SIDE
    far_up = pick(ups, opposite)
    for way, step in ((0, 1), (1, 3)):
        sender = (t + 4 - step) % SIDE

        def send_one(n, held, slot, way=way):
            table[SEND + 24 * way + at_one(ways[way], t, n)] = held

        each(t, t + step, send_one)

        def relay(j, _, way=way, sender=sender):
            table[SEND + 24 * way + pick(ways[way]["relay"], t) + j] = RELAY + at_two(ways[way], sender, j)
            return 0

        lax.fori_loop(0, pick(ways[way]["two"], sender), relay, 0)

        def take_one(n, held, slot, way=way, sender=sender):
            table[TAKE + 24 * way + at_one(ways[way], sender, n)] = slot

        each(sender, t, take_one)

    def take_two(n, held, slot):
        @pl.when(n < far_up)
        def _():
            table[TAKE + pick(ways[0]["relay"], (t + 3) % SIDE) + n] = slot

        @pl.when(n >= far_up)
        def _():
            table[TAKE + 24 + pick(ways[1]["relay"], (t + 1) % SIDE) + n - far_up] = slot

    each(opposite, t, take_two)

    def near(n, held, slot):
        table[NEAR + n] = held * 32 + slot

    table[1] = each(t, t, near)


def plan(lists, where):
    smem = pl.BlockSpec(memory_space=pltpu.SMEM)
    return pl.pallas_call(
        plan_kernel,
        out_shape=jax.ShapeDtypeStruct((256,), jnp.int32),
        in_specs=[smem, smem],
        out_specs=smem,
        scratch_shapes=[pltpu.SMEM((N_AO, LIST), jnp.int32)],
    )(lists, where)


def pack_kernel(step, held, relays, table, *refs):
    refs = list(refs)
    tiles = {m: [refs.pop(0) for _ in range(CHUNKS)] for m in held}
    came = [refs.pop(0) for _ in range(2 * relays)]
    up, down, room, sems = refs
    arrivals, leavings = [], []
    for way, out in enumerate((up, down)):
        for h in range(G):
            k = G * way + h
            code = table[SEND + 24 * way + G * step + h]
            dst = room.at[k]

            @pl.when(code < RELAY)
            def _(code=code, dst=dst, k=k):
                for m in held:
                    for c, tile in enumerate(tiles[m]):
                        @pl.when(code // PER == m * CHUNKS + c)
                        def _():
                            pltpu.make_async_copy(tile.at[code % PER], dst, sems.at[k]).start()

            @pl.when(code >= RELAY)
            def _(code=code, dst=dst, k=k, way=way):
                for q in range(relays):
                    @pl.when((code - RELAY) // G == q)
                    def _():
                        pltpu.make_async_copy(came[2 * q + way].at[(code - RELAY) % G], dst, sems.at[k]).start()

            arrivals.append(pltpu.make_async_copy(tiles[0][0].at[0], dst, sems.at[k]))
            leavings.append(pltpu.make_async_copy(dst, out.at[h], sems.at[2 * G + k]))
    for arrival, leaving in zip(arrivals, leavings):
        arrival.wait()
        leaving.start()
    for leaving in leavings:
        leaving.wait()


def pack(step, table, tiles, came):
    relays = max(step - DELAY + 1, 0)
    held = [m for m in ORDER if G * step >= FIRST or m != FAR]
    smem = pl.BlockSpec(memory_space=pltpu.SMEM)
    hbm = pl.BlockSpec(memory_space=pl.ANY)
    operands = [chunk for m in held for chunk in tiles[m]]
    for q in range(relays):
        operands += came[q]
    shape = jax.ShapeDtypeStruct((G, BS, WIDE), jnp.bfloat16)
    return pl.pallas_call(
        functools.partial(pack_kernel, step, held, relays),
        out_shape=[shape, shape],
        in_specs=[smem] + [hbm] * len(operands),
        out_specs=[hbm, hbm],
        scratch_shapes=[pltpu.VMEM((2 * G, BS, WIDE), jnp.bfloat16), pltpu.SemaphoreType.DMA((4 * G,))],
        cost_estimate=pl.CostEstimate(flops=0, bytes_accessed=1024, transcendentals=0),
    )(table, *operands)


def gather(own_c, left, right, sems, wanted):
    n = jnp.int32(0)
    for ok, slot, start in wanted:
        @pl.when(ok)
        def _(n=n, slot=slot, start=start):
            at = pl.ds(pl.multiple_of(n * BS, BS), BS)
            pltpu.make_async_copy(own_c.at[:, slot // 2, slot % 2], left.at[:, :, at], sems.at[0]).start()
            start(right.at[at], sems.at[1])
        n = n + jnp.where(ok, 1, 0)
    return n


def arrive(own_c, left, right, sems, n):
    def one(_, carry):
        at = pl.ds(0, BS)
        pltpu.make_async_copy(own_c.at[:, 0, 0], left.at[:, :, at], sems.at[0]).wait()
        pltpu.make_async_copy(right.at[at], right.at[at], sems.at[1]).wait()
        return carry

    lax.fori_loop(0, n, one, 0)

    @pl.when(n % 2 == 1)
    def _():
        at = pl.ds(pl.multiple_of(n * BS, BS), BS)
        left[:, :, at] = jnp.zeros((NB, BS, BS), jnp.bfloat16)
        right[at, :] = jnp.zeros((BS, WIDE), jnp.bfloat16)


def contract(left, right, n, acc, cols):
    def pair(p, carry):
        at = pl.ds(pl.multiple_of(p * 2 * BS, 2 * BS), 2 * BS)
        acc[:, cols] += jnp.dot(
            left[:, :, at].reshape(ROWS, 2 * BS), right[at, cols], preferred_element_type=jnp.float32
        )
        return carry

    lax.fori_loop(0, (n + 1) // 2, pair, 0)


def from_steps(table, steps, came):
    wanted = []
    for q, step in enumerate(steps):
        for way in range(2):
            for h in range(G):
                slot = table[TAKE + 24 * way + G * step + h]

                def start(dst, sem, q=q, way=way, h=h):
                    pltpu.make_async_copy(came[2 * q + way].at[h], dst, sem).start()

                wanted.append((slot >= 0, jnp.maximum(slot, 0), start))
    return wanted


def sum_kernel(near, steps, clear, table, own_c, *refs):
    refs = list(refs)
    before = None if clear else refs.pop(0)
    tiles = {m: [refs.pop(0) for _ in range(CHUNKS)] for m in near}
    came = [refs.pop(0) for _ in range(2 * len(steps))]
    out, left, right, acc, sems = refs
    wanted = from_steps(table, steps, came)
    for s in range(2 * SIDE if near else 0):
        entry = table[NEAR + s]
        code = entry // 32
        here = jnp.bool_(False)
        for m in near:
            here = jnp.logical_or(here, code // NB == m)

        def start(dst, sem, code=code):
            for m in near:
                for c, chunk in enumerate(tiles[m]):
                    @pl.when(code // PER == m * CHUNKS + c)
                    def _():
                        pltpu.make_async_copy(chunk.at[code % PER], dst, sem).start()

        wanted.append((jnp.logical_and(s < table[1], here), entry % 32, start))
    n = gather(own_c, left, right, sems, wanted)
    parts = [slice(j * WIDE // PARTS, (j + 1) * WIDE // PARTS) for j in range(PARTS)]
    fetches = []
    for j, cols in enumerate(parts):
        if clear:
            acc[:, cols] = jnp.zeros((ROWS, WIDE // PARTS), jnp.float32)
        else:
            copy = pltpu.make_async_copy(before.at[:, cols], acc.at[:, cols], sems.at[2 + j])
            copy.start()
            fetches.append(copy)
    arrive(own_c, left, right, sems, n)
    stores = []
    for j, cols in enumerate(parts):
        if not clear:
            fetches[j].wait()
        contract(left, right, n, acc, cols)
        copy = pltpu.make_async_copy(acc.at[:, cols], out.at[:, cols], sems.at[2 + j])
        copy.start()
        stores.append(copy)
    for copy in stores:
        copy.wait()


def last_kernel(steps, table, own_c, before, turn, first, second, *refs):
    came = refs[:2 * len(steps)]
    out, left, right, acc, rows, part, mixed, total, sems = refs[2 * len(steps):]
    fetches = []
    for j in range(PARTS):
        cols = pl.ds(j * WIDE // PARTS, WIDE // PARTS)
        fetches.append(pltpu.make_async_copy(before.at[:, cols], acc.at[:, cols], sems.at[2 + j]))
    fetches[0].start()
    n = gather(own_c, left, right, sems, from_steps(table, steps, came))
    for copy in fetches[1:]:
        copy.start()
    own = []
    for c, chunk in enumerate((first, second)):
        copy = pltpu.make_async_copy(chunk, rows.at[pl.ds(c * PER, PER)], sems.at[2 + PARTS + c])
        copy.start()
        own.append(copy)
    arrive(own_c, left, right, sems, n)
    pairs = (n + 1) // 2
    for j, fetch in enumerate(fetches):
        fetch.wait()
        cols = slice(j * WIDE // PARTS, (j + 1) * WIDE // PARTS)

        @pl.when(pairs == 0)
        def _():
            part[:, cols] = acc[:, cols].astype(jnp.bfloat16)

        for p in range(1, G * len(steps) + 1):
            @pl.when(pairs == p)
            def _():
                added = jnp.dot(
                    left[:, :, :2 * p * BS].reshape(ROWS, 2 * p * BS), right[:2 * p * BS, cols],
                    preferred_element_type=jnp.float32,
                )
                part[:, cols] = (acc[:, cols] + added).astype(jnp.bfloat16)

        for k in range(WIDE // PARTS // 256):
            here = slice(cols.start + k * 256, cols.start + (k + 1) * 256)
            mixed[:, here] = jnp.dot(
                part[:, here], turn[...], preferred_element_type=jnp.float32
            ).astype(jnp.bfloat16)

    for copy in own:
        copy.wait()
    total[...] = jnp.zeros_like(total)

    @pl.loop(0, ROWS // 32, unroll=4)
    def _(j):
        def stacked(load):
            halves = []
            for h in range(2):
                at = pl.multiple_of(j * 32 + h * 16, 16)
                halves.append(jnp.concatenate([load(at, slice(p * BS, (p + 1) * BS)) for p in range(AB)], axis=0))
            return jnp.concatenate(halves, axis=1)

        block = j // (BS // 32)
        total[...] += lax.dot_general(
            stacked(lambda at, cols: mixed[pl.ds(at, 16), cols]),
            stacked(lambda at, cols: rows[block, pl.ds(pl.multiple_of(at - block * BS, 16), 16), cols]),
            (((1,), (1,)), ((), ())),
            preferred_element_type=jnp.float32,
        )

    r = lax.broadcasted_iota(jnp.int32, (256, 256), 0)
    c = lax.broadcasted_iota(jnp.int32, (256, 256), 1)
    kept = jnp.where(r % 16 == c % 16, total[...], 0.0)
    kept = kept.reshape(16, 16, 256).sum(axis=1)
    rr = lax.broadcasted_iota(jnp.int32, (256, 16), 0)
    cc = lax.broadcasted_iota(jnp.int32, (256, 16), 1)
    pick_q = jnp.where(rr // 16 == cc, 1.0, 0.0)
    out[...] = jnp.dot(kept, pick_q, preferred_element_type=jnp.float32, precision=lax.Precision.HIGHEST)


def run(kernel, table, own_c, operands, vmem_operands, blocks, last):
    smem = pl.BlockSpec(memory_space=pltpu.SMEM)
    vmem = pl.BlockSpec(memory_space=pltpu.VMEM)
    hbm = pl.BlockSpec(memory_space=pl.ANY)
    scratch = [
        pltpu.VMEM((NB, BS, blocks * BS), jnp.bfloat16),
        pltpu.VMEM((blocks * BS, WIDE), jnp.bfloat16),
        pltpu.VMEM((ROWS, WIDE), jnp.float32),
    ]
    if last:
        scratch += [
            pltpu.VMEM((NB, BS, WIDE), jnp.bfloat16),
            pltpu.VMEM((ROWS, WIDE), jnp.bfloat16),
            pltpu.VMEM((ROWS, WIDE), jnp.bfloat16),
            pltpu.VMEM((256, 256), jnp.float32),
        ]
    scratch.append(pltpu.SemaphoreType.DMA((4 + PARTS,)))
    shape = (16, 16) if last else (ROWS, WIDE)
    return pl.pallas_call(
        kernel,
        out_shape=jax.ShapeDtypeStruct(shape, jnp.float32),
        in_specs=[smem, hbm] + [vmem if k in vmem_operands else hbm for k in range(len(operands))],
        out_specs=vmem if last else hbm,
        scratch_shapes=scratch,
        compiler_params=pltpu.CompilerParams(vmem_limit_bytes=VMEM_BYTES),
        cost_estimate=pl.CostEstimate(flops=0, bytes_accessed=1024, transcendentals=0),
    )(table, own_c, *operands)


def flatten_kernel(tile, out):
    out[0] = tile[0, 0, 0].reshape(BS, WIDE)


def flatten(integrals, chunk):
    return pl.pallas_call(
        flatten_kernel,
        grid=(PER,),
        out_shape=jax.ShapeDtypeStruct((PER, BS, WIDE), jnp.bfloat16),
        in_specs=[pl.BlockSpec((1, 1, 1, BS, AB, BS), lambda b: (0, 0, chunk * PER + b, 0, 0, 0))],
        out_specs=pl.BlockSpec((1, BS, WIDE), lambda b: (b, 0, 0)),
        cost_estimate=pl.CostEstimate(flops=0, bytes_accessed=8 * 1024 * 1024, transcendentals=0),
    )(integrals)


def per_device(integrals, block_list, pair_count, occupied, virtual):
    own_c = occupied[0]
    ao = lax.axis_index("ao")
    aux = lax.axis_index("aux")
    where = jnp.stack([ao, aux]).astype(jnp.int32)

    own = [flatten(integrals, 0)]
    lists = jnp.concatenate([block_list.reshape(1, 32), pair_count], axis=1)
    own[0], lists = lax.optimization_barrier((own[0], lists))
    lists = jnp.concatenate([lists, around(lists, 1)], axis=0)
    integrals, lists = lax.optimization_barrier((integrals, lists))
    own.append(flatten(integrals, 1))
    lists = jnp.concatenate([lists, around(lists, 2)], axis=0)
    lists = lax.ppermute(lists, "aux", [(g, g ^ 1) for g in range(8)])
    lists = jnp.concatenate([lists, around(lists, 1)], axis=0)
    lists = jnp.concatenate([lists, around(lists, 2)], axis=0)
    table = plan(lists, where)
    longest = table[0]

    last = [across(own[c], 1) for c in range(CHUNKS)]
    following = [across(own[c], -1) for c in range(CHUNKS)]
    first, _, table = lax.optimization_barrier((last[0], following[0], table))
    far = [across(first, 1), across(following[1], -1)]
    tiles = [own, following, far, last]

    came = []

    def add(acc, near, some):
        blocks = [chunk for tile in near for chunk in tiles[tile]] + [b for q in some for b in came[q]]
        return run(
            functools.partial(sum_kernel, near, some, acc is None), table, own_c,
            ([] if acc is None else [acc]) + blocks, (), 2 * SIDE + 2 * G * len(some), False,
        )

    acc = add(None, (0, 1, 3), ())
    table, acc = lax.optimization_barrier((table, acc))
    for q in range(ALWAYS):
        up, down = pack(q, table, tiles, came)
        if q == 0:
            up, down, table, far[0] = lax.optimization_barrier((up, down, table, far[0]))
        if q == ALWAYS - 1:
            up, down, acc = lax.optimization_barrier((up, down, acc))
            acc = add(acc, (FAR,), tuple(range(q - 1)))
        came.append(list(lax.optimization_barrier((around(up, 1), around(down, -1)))))
    acc = add(acc, (), (ALWAYS - 2,))

    block = virtual[0]
    zero = jnp.zeros_like(block)
    turn = jnp.concatenate(
        [jnp.concatenate([block, zero], axis=1), jnp.concatenate([zero, block], axis=1)], axis=0
    )

    def finish(some, came, acc, turn):
        return run(
            functools.partial(last_kernel, some), table, own_c,
            [acc, turn] + own + [b for q in some for b in came[q]], (1,), 2 * G * len(some), True,
        )

    def ending(extra):
        def branch(came, acc, turn):
            came = list(came)
            for q in range(ALWAYS, ALWAYS + extra):
                up, down = pack(q, table, tiles, came)
                came.append([around(up, 1), around(down, -1)])
            return finish(tuple(range(ALWAYS - 1, ALWAYS + extra)), came, acc, turn)
        return branch

    more = (longest > G * ALWAYS).astype(jnp.int32) + (longest > G * (ALWAYS + 1)).astype(jnp.int32)
    partial = lax.switch(more, [ending(extra) for extra in range(STEPS - ALWAYS + 1)], came, acc, turn)

    pieces = lax.all_to_all(partial.reshape(128, 2), AXES, split_axis=0, concat_axis=0, tiled=True)
    return pieces.sum(axis=0).reshape(1, 2)


def solution(mesh):
    placed = (
        P("ao", "aux", None, None, None, None),
        P("ao", None, None),
        P("ao", None),
        P("ao", None, None, None, None, None),
        P("aux", None, None),
    )
    return jax.shard_map(
        per_device, mesh=mesh, in_specs=placed, out_specs=P("ao", "aux"), check_vma=False
    )
```
